256 devices in a mesh: pair: 64 (over y, z, core), virt: 4 (over x).
Axes of the slice: x: 4, y: 4, z: 8, core: 2. Of those that a mesh axis runs over, the one named last changes fastest.
Arguments:
- amplitudes: bfloat16 [256, 512, 512], P('pair', 'virt'), may hold values from -6 to 6
- panels: bfloat16 [16, 512, 512], P('virt', 'pair'), may hold values from -0.125 to 0.125
- domain: int32 [256, 8, 8], P('pair'), may hold values 0 or 1
- mirror: int32 [256], P('pair'), may hold values from 0 to 255, as said below
Outputs:
- symmetrized: float32 [256, 512, 512], P('pair', None, 'virt')
The draws below stay inside these ranges and needn't reach their ends.
Inputs may be any that keep to these rules, and one draw needn't show every extreme that they name: mirror is an involution without fixed points; a pair of group g (pairs g * 4 to g * 4 + 3) has its mirror in group g XOR (32), and the pairs of each such couple of groups correspond one to one.
All inputs are finite; a program needn't handle non-finite values. No bound on the sum of `domain` on one device may be relied on, other than what follows from the above.
Results may differ from the reference program's by a relative error of at most 0.0029.
Values may be sent and summed in bfloat16 or wider, within the bound.
A program may use at most 64 MiB of HBM per device.

```python
import jax
import jax.numpy as jnp
from jax import lax

TILE = 64
NT = 8
NQ = 16
PAIR_DEV = 4
VW = 512
PAIRS = 256
N_PAIR = 64


def draw_mirror(key, part):
    key = jax.random.fold_in(key, 11)
    group_half = N_PAIR // 2
    key_list = jax.random.split(key, group_half)
    perm_table = jax.vmap(lambda single_key: jax.random.permutation(single_key, PAIR_DEV))(key_list).astype(jnp.int32)
    group_ids = jnp.arange(group_half, dtype=jnp.int32)[:, None]
    low_side = (group_ids + group_half) * PAIR_DEV + perm_table
    inverse = jnp.argsort(perm_table, axis=1, stable=True).astype(jnp.int32)
    high_side = group_ids * PAIR_DEV + inverse
    return jnp.concatenate([low_side.reshape(-1), high_side.reshape(-1)])


def place_ends(array, own_key, least, high):
    longest = array.shape.index(max(array.shape))
    spots = []
    for shift in (0, 1):
        where = [jax.random.randint(jax.random.fold_in(own_key, axis), (), 0, length) for axis, length in enumerate(array.shape)]
        where[longest] = (where[longest] + shift) % array.shape[longest]
        spots.append(tuple(where))
    return array.at[spots[0]].set(least).at[spots[1]].set(high)


def level_of(own_key, shape, shards, least, high):
    def one(axis_at, blocks):
        steps = jax.random.uniform(jax.random.fold_in(jax.random.fold_in(own_key, 6), axis_at), (blocks,), jnp.float32, least / len(shards), high / len(shards))
        return jnp.repeat(jnp.exp(steps), shape[axis_at] // blocks).reshape((-1,) + (1,) * (len(shape) - axis_at - 1))

    loudness = one(*shards[0])
    for cut in shards[1:]:
        loudness = loudness * one(*cut)
    return loudness


def scatter_about(own_key, shape, scale, bound, shards=(), kind=jnp.bfloat16):
    values = jax.random.normal(own_key, shape, jnp.float32) * scale
    if len(shards) > 0:
        values = level_of(own_key, shape, shards, -0.22, 0.18) * values
    return jnp.clip(values, min=-bound, max=bound).astype(kind)


def setup_inputs(seed: int = 0) -> dict:
    streams_of = jax.random.split(jax.random.key(seed), 5)
    amplitudes = scatter_about(streams_of[0], (PAIRS, VW, VW), 1.0, 6.0, ((0, 64), (1, 4)))
    panels = scatter_about(streams_of[1], (NQ, VW, VW), (4 * VW) ** -0.5, 0.125, ((0, 4), (1, 64)))
    domain = place_ends((jax.random.randint(streams_of[2], (PAIRS, NT, NT), 0, 2) < 1).astype(jnp.int32), jax.random.fold_in(streams_of[2], 1), 0, 1)
    mirror = draw_mirror(jax.random.fold_in(streams_of[4], 71), 0)
    return dict(amplitudes=amplitudes, panels=panels, domain=domain, mirror=mirror)


def expand_mask(domain_tiles):
    lead_shape = domain_tiles.shape[:-2]
    tile_count = domain_tiles.shape[-1]
    spread = jnp.broadcast_to(domain_tiles[..., :, None, :, None], lead_shape + (tile_count, TILE, tile_count, TILE))
    return spread.reshape(lead_shape + (tile_count * TILE, tile_count * TILE))


def ladder_pair(inputs, panels_wide):
    amplitude, domain_tiles = inputs
    masked = amplitude.astype(jnp.float32) * expand_mask(domain_tiles).astype(jnp.float32)
    half_done = jnp.einsum("cd,qbd->qcb", masked, panels_wide)
    stored = lax.optimization_barrier(half_done.astype(jnp.bfloat16))
    return jnp.einsum("qac,qcb->ab", panels_wide, stored.astype(jnp.float32))


def reference(amplitudes, panels, domain, mirror):
    panels_wide = panels.astype(jnp.float32)
    residual = lax.map(lambda inputs: ladder_pair(inputs, panels_wide), (amplitudes, domain))
    partner = jnp.take(residual, mirror, axis=0)
    mask_full = expand_mask(domain).astype(jnp.float32)
    return mask_full * (residual + jnp.transpose(partner, (0, 2, 1)))
```

```python
import functools

import jax
import jax.numpy as jnp
from jax import lax
from jax.experimental import pallas as pl
from jax.experimental.pallas import tpu as pltpu
from jax.sharding import PartitionSpec as P

MESH = pl.DeviceIdType.MESH
NX, NY, NZ = 4, 4, 8
PAIRS_DEV, VW, TILE = 4, 512, 64
ROWS = VW // NX
TILES_B = ((1, 2), (1, 1))
TILES_C = ((3, 1), (2, 2))
F32, BF16 = jnp.float32, jnp.bfloat16


def dot_t(a, b):
    return lax.dot_general(a, b, (((1,), (1,)), ((), ())), preferred_element_type=F32)


class Slots:
    def __init__(self):
        self.names = {}

    def __getitem__(self, name):
        return self.names.setdefault(name, len(self.names))


def kernel(slots, amp_ref, pan_ref, dom_ref, mir_ref, out_ref,
           stg, xbuf, pst, bb, tacc, trecv, sout, land_low, land_up, send_sem, recv_sem, loc_sem):
    x = lax.axis_index("virt")
    p = lax.axis_index("pair")
    c = p % 2
    z = (p // 2) % NZ
    y = p // (2 * NZ)
    half = y // 2
    ybase = y % 2

    def dev(x_, y_, z_, c_):
        return ((y_ * NZ + z_) * 2 + c_, x_)

    def off(dx=0, dy=0, dz=0):
        return dev((x + dx) % NX, (y + dy) % NY, (z + dz) % NZ, c)

    sibling = dev(x, y, z, 1 - c)
    started = []

    def copy(src, dst, name, device):
        k = slots[name]
        return pltpu.make_async_remote_copy(
            src_ref=src, dst_ref=dst, send_sem=send_sem.at[k], recv_sem=recv_sem.at[k],
            device_id=device, device_id_type=MESH)

    def send(ref, name, device):
        cp = copy(ref, ref, name, device)
        cp.start()
        started.append(cp)

    def arrive(ref, name):
        copy(ref, ref, name, sibling).wait_recv()

    barrier = pltpu.get_barrier_semaphore()
    peers = [off(dz=d) for d in range(1, NZ)] + [off(dy=1), off(dy=3)]
    peers += [dev((x + dx) % NX, (y + dy) % NY, z, (c + dc) % 2)
              for dx in range(NX) for dy in (0, 2) for dc in range(2) if (dx, dy, dc) != (0, 0, 0)]
    for peer in peers:
        pl.semaphore_signal(barrier, inc=1, device_id=peer, device_id_type=MESH)
    pl.semaphore_wait(barrier, len(peers))

    k = slots["swap"]
    swap = pltpu.make_async_remote_copy(
        src_ref=pan_ref.at[1 - c], dst_ref=pst, send_sem=send_sem.at[k], recv_sem=recv_sem.at[k],
        device_id=sibling, device_id_type=MESH)
    swap.start()

    lane = lax.broadcasted_iota(jnp.int32, (1, 128), 1)
    order = []
    for i in range(PAIRS_DEV):
        found = jnp.int32(0)
        for q in range(PAIRS_DEV):
            found = jnp.where(mir_ref[q] % PAIRS_DEV == i, jnp.int32(q), found)
        order.append(jnp.where(half == 0, jnp.int32(i), found))
    for i in range(PAIRS_DEV):
        for h in range(2):
            row = 2 * x + h
            parts = [jnp.where(lane < TILE, dom_ref[order[i], row, 2 * t], dom_ref[order[i], row, 2 * t + 1])
                     for t in range(4)]
            mask = jnp.concatenate(parts, axis=1).astype(F32)
            rows = pl.ds(h * TILE, TILE)
            stg[i, rows, :] = (amp_ref[order[i], rows, :].astype(F32) * mask).astype(BF16)

    swap.wait()
    mine = pan_ref[c].astype(F32)
    other = pst[...].astype(F32)
    first = jnp.where(c == 0, mine, other)
    second = jnp.where(c == 0, other, mine)
    for j in range(2):
        rows16 = jnp.concatenate([first[8 * j:8 * j + 8], second[8 * j:8 * j + 8]], axis=0).astype(BF16)
        for t in range(4):
            bb[t, x, j, y, z] = rows16[:, 128 * t:128 * t + 128]

    def z1(z_):
        return bb.at[pl.ds(1, 3), x, :, y, z_]

    def x1(x_):
        return bb.at[0, x_, :, y, z]

    def y2(y_):
        return bb.at[0, :, :, y_, z]

    def ring_a(j, z_, part=None):
        return bb.at[0, slice(None) if part is None else pl.ds(2 * part, 2), j, :, z_]

    def line_b(j, x_):
        return bb.at[pl.ds(*TILES_B[j]), x_, j, y]

    def ring_b(j, y_, part=None):
        return bb.at[pl.ds(*TILES_B[j]), slice(None) if part is None else pl.ds(2 * part, 2), j, y_]

    def line_c(j, y_):
        return bb.at[pl.ds(*TILES_C[j]), x, j, y_]

    def ring_c(j, x_, part=None):
        return bb.at[pl.ds(*TILES_C[j]), x_, j, slice(None) if part is None else pl.ds(2 * part, 2)]

    for d in range(1, NX):
        send(x1(x), ("x1", d), off(dx=d))
    for d in (1, 7, 2, 6, 3, 5, 4):
        send(z1(z), ("z1", d), off(dz=d))

    def amp_slot(x_):
        return xbuf.at[half, pl.ds(pl.multiple_of(x_ * ROWS, ROWS), ROWS), :]

    for i in range(PAIRS_DEV):
        k = slots[("amp_s", i)]

        @pl.when(jnp.logical_not(jnp.logical_and(half == c, x == i)))
        def _():
            pltpu.make_async_remote_copy(
                src_ref=stg.at[i], dst_ref=amp_slot(x), send_sem=send_sem.at[k],
                recv_sem=recv_sem.at[slots[("amp", 0)] + x],
                device_id=dev(i, ybase + 2 * c, z, half), device_id_type=MESH).start()

        @pl.when(jnp.logical_and(half == c, x == i))
        def _():
            pltpu.make_async_copy(stg.at[i], amp_slot(x), loc_sem.at[0]).start()

    for d in range(1, NX):
        arrive(x1((x - d) % NX), ("x1", d))
    for d in range(1, NY):
        send(y2(y), ("y2", d), off(dy=d))
    for d in (1, 7, 2, 6, 3, 5, 4):
        arrive(z1((z - d) % NZ), ("z1", d))
    for j in range(2):
        for d in range(1, 4):
            send(line_b(j, x), ("lb", j, d), off(dx=d))
            send(line_c(j, y), ("lc", j, d), off(dy=d))

    for d in range(1, NY):
        arrive(y2((y - d) % NY), ("y2", d))

    def a_step(j, s):
        if s > 1:
            arrive(ring_a(j, (z - s + 1) % NZ), ("ra", j, 1, s - 1))
        send(ring_a(j, (z - s + 1) % NZ, 0 if s == 4 else None), ("ra", j, 1, s), off(dz=1))
        if s > 1:
            arrive(ring_a(j, (z + s - 1) % NZ), ("ra", j, 7, s - 1))
        send(ring_a(j, (z + s - 1) % NZ, 1 if s == 4 else None), ("ra", j, 7, s), off(dz=7))

    def b_step(j, s):
        if s == 1:
            for d in range(1, 4):
                arrive(line_b(j, (x - d) % NX), ("lb", j, d))
            for d in (1, 3):
                send(ring_b(j, y), ("rb", j, d, 1), off(dy=d))
        else:
            for d in (1, 3):
                arrive(ring_b(j, (y - d) % NY), ("rb", j, d, 1))
                send(ring_b(j, (y - d) % NY, d // 2), ("rb", j, d, 2), off(dy=d))

    def c_step(j, s):
        if s == 1:
            for d in range(1, 4):
                arrive(line_c(j, (y - d) % NY), ("lc", j, d))
            for d in (1, 3):
                send(ring_c(j, x), ("rc", j, d, 1), off(dx=d))
        else:
            for d in (1, 3):
                arrive(ring_c(j, (x - d) % NX), ("rc", j, d, 1))
                send(ring_c(j, (x - d) % NX, d // 2), ("rc", j, d, 2), off(dx=d))

    a_step(0, 1)
    a_step(1, 1)

    def amp_arrived(slot, x_):
        return xbuf.at[slot, pl.ds(x_ * ROWS, ROWS), :]

    for x_ in range(NX):
        here = amp_arrived(c, x_)

        @pl.when(jnp.logical_not(jnp.logical_and(half == c, x == x_)))
        def _():
            copy(here, here, ("amp", x_), sibling).wait_recv()

        @pl.when(jnp.logical_and(half == c, x == x_))
        def _():
            pltpu.make_async_copy(stg.at[0], here, loc_sem.at[0]).wait()

        send(here, ("fwd", x_), sibling)

    b_step(0, 1)
    c_step(0, 1)
    a_step(0, 2)
    a_step(1, 2)
    b_step(1, 1)
    c_step(1, 1)
    a_step(0, 3)
    a_step(1, 3)
    b_step(0, 2)
    c_step(0, 2)
    a_step(0, 4)
    a_step(1, 4)
    b_step(1, 2)
    c_step(1, 2)

    def last(j):
        arrive(ring_a(j, (z + 4) % NZ, 0), ("ra", j, 1, 4))
        arrive(ring_a(j, (z + 4) % NZ, 1), ("ra", j, 7, 4))
        for d in (1, 3):
            arrive(ring_b(j, (y + 2) % NY, d // 2), ("rb", j, d, 2))
            arrive(ring_c(j, (x + 2) % NX, d // 2), ("rc", j, d, 2))

    for x_ in range(NX):
        arrive(amp_arrived(1 - c, x_), ("fwd", x_))

    tacc[...] = jnp.zeros_like(tacc)
    for j in range(2):
        last(j)

        @pl.loop(0, NX)
        def _(x_):
            panel = jnp.concatenate([bb[t, x_, j].reshape(VW, 128) for t in range(4)], axis=1)
            done = dot_t(xbuf[0], panel).astype(BF16)
            tacc[...] += jnp.dot(panel, done, preferred_element_type=F32)
            turned = dot_t(panel, xbuf[1]).astype(BF16)
            tacc[...] += dot_t(turned, panel)

    k = slots["tswap"]
    tswap = pltpu.make_async_remote_copy(
        src_ref=tacc.at[pl.ds(pl.multiple_of((1 - c) * 256, 256), 256), :], dst_ref=trecv,
        send_sem=send_sem.at[k], recv_sem=recv_sem.at[k], device_id=sibling, device_id_type=MESH)
    tswap.start()
    tswap.wait()
    full = (tacc[pl.ds(pl.multiple_of(c * 256, 256), 256), :] + trecv[...]).astype(BF16)
    for t in range(4):
        sout[t] = full[:, 128 * t:128 * t + 128]

    def low_dst(i, c_):
        return land_low.at[i, pl.ds(pl.multiple_of(c_ * 256, 256), 256), :]

    for t in range(NX):
        k = slots[("low_s", t)]
        self_ = jnp.logical_and(jnp.logical_and(half == 0, c == 0), x == t)

        @pl.when(jnp.logical_not(self_))
        def _():
            pltpu.make_async_remote_copy(
                src_ref=sout.at[t], dst_ref=low_dst(x, c), send_sem=send_sem.at[k],
                recv_sem=recv_sem.at[slots[("low", 0)] + 2 * x + c],
                device_id=dev(t, ybase, z, half), device_id_type=MESH).start()

        @pl.when(self_)
        def _():
            pltpu.make_async_copy(sout.at[t], low_dst(x, c), loc_sem.at[1]).start()

    for h in range(2):
        k = slots[("up_s", h)]
        to = 2 * c + h
        self_ = jnp.logical_and(jnp.logical_and(half == 1, c == 1), x == to)

        @pl.when(jnp.logical_not(self_))
        def _():
            pltpu.make_async_remote_copy(
                src_ref=sout.at[:, pl.ds(128 * h, 128), :], dst_ref=land_up.at[x], send_sem=send_sem.at[k],
                recv_sem=recv_sem.at[slots[("up", 0)] + x],
                device_id=dev(to, ybase + 2, z, half), device_id_type=MESH).start()

        @pl.when(self_)
        def _():
            pltpu.make_async_copy(sout.at[:, pl.ds(128 * h, 128), :], land_up.at[x], loc_sem.at[1]).start()

    def mask_cols(i):
        return [jnp.where(lane < TILE, dom_ref[i, r, 2 * x], dom_ref[i, r, 2 * x + 1]).astype(F32) for r in range(8)]

    @pl.when(half == 0)
    def _():
        for i in range(PAIRS_DEV):
            for c_ in range(2):
                here = land_low.at[i, pl.ds(c_ * 256, 256), :]
                self_ = jnp.logical_and(jnp.logical_and(c == 0, x == i), c_ == 0)

                @pl.when(jnp.logical_not(self_))
                def _():
                    copy(here, here, ("low", i, c_), sibling).wait_recv()

                @pl.when(self_)
                def _():
                    pltpu.make_async_copy(sout.at[0], here, loc_sem.at[1]).wait()

            masks = mask_cols(i)
            for r in range(8):
                rows = pl.ds(r * TILE, TILE)
                out_ref[i, rows, :] = land_low[i, rows, :].astype(F32) * masks[r]

    @pl.when(half == 1)
    def _():
        for i in range(PAIRS_DEV):
            self_ = jnp.logical_and(c == 1, jnp.logical_and(x == i, x // 2 == 1))

            @pl.when(jnp.logical_not(self_))
            def _():
                copy(land_up.at[i], land_up.at[i], ("up", i), sibling).wait_recv()

            @pl.when(self_)
            def _():
                pltpu.make_async_copy(sout.at[:, pl.ds(0, 128), :], land_up.at[i], loc_sem.at[1]).wait()

        for i in range(PAIRS_DEV):
            masks = mask_cols(i)
            got = land_up[mir_ref[i] % PAIRS_DEV].astype(F32)
            for t in range(4):
                turned = got[t].T
                for h in range(2):
                    out_ref[i, pl.ds(128 * t + TILE * h, TILE), :] = turned[TILE * h:TILE * h + TILE] * masks[2 * t + h]

    for cp in started:
        cp.wait_send()
    for i in range(PAIRS_DEV):
        @pl.when(jnp.logical_not(jnp.logical_and(half == c, x == i)))
        def _():
            copy(stg.at[i], stg.at[i], ("amp_s", i), sibling).wait_send()
    for t in range(NX):
        @pl.when(jnp.logical_not(jnp.logical_and(jnp.logical_and(half == 0, c == 0), x == t)))
        def _():
            copy(sout.at[t], sout.at[t], ("low_s", t), sibling).wait_send()
    for h in range(2):
        @pl.when(jnp.logical_not(jnp.logical_and(jnp.logical_and(half == 1, c == 1), x == 2 * c + h)))
        def _():
            part = sout.at[:, pl.ds(128 * h, 128), :]
            copy(part, part, ("up_s", h), sibling).wait_send()


def body(amplitudes, panels, domain, mirror):
    slots = Slots()
    for i in range(NX):
        slots[("amp", i)]
    for i in range(NX):
        for c_ in range(2):
            slots[("low", i, c_)]
    slots.names[("low", 0)] = slots[("low", 0, 0)]
    for i in range(NX):
        slots[("up", i)]
    vm = pl.BlockSpec(memory_space=pltpu.VMEM)
    sm = pl.BlockSpec(memory_space=pltpu.SMEM)
    return pl.pallas_call(
        functools.partial(kernel, slots),
        out_shape=jax.ShapeDtypeStruct((PAIRS_DEV, VW, ROWS), F32),
        in_specs=[vm, vm, sm, sm],
        out_specs=vm,
        scratch_shapes=[
            pltpu.VMEM((PAIRS_DEV, ROWS, VW), BF16),
            pltpu.VMEM((2, VW, VW), BF16),
            pltpu.VMEM((16, VW), BF16),
            pltpu.VMEM((4, NX, 2, NY, NZ, 16, 128), BF16),
            pltpu.VMEM((VW, VW), F32),
            pltpu.VMEM((256, VW), F32),
            pltpu.VMEM((4, 256, 128), BF16),
            pltpu.VMEM((PAIRS_DEV, VW, ROWS), BF16),
            pltpu.VMEM((PAIRS_DEV, 4, 128, 128), BF16),
            pltpu.SemaphoreType.DMA((160,)),
            pltpu.SemaphoreType.DMA((160,)),
            pltpu.SemaphoreType.DMA((2,)),
        ],
        name="ladder",
        cost_estimate=pl.CostEstimate(flops=8 * 2**30, bytes_accessed=2 * 2**20, transcendentals=0),
        compiler_params=pltpu.CompilerParams(collective_id=0, has_side_effects=True, vmem_limit_bytes=48 * 2**20),
    )(amplitudes, panels.reshape(2, 16, VW), domain, mirror)


def solution(mesh):
    in_specs = (P("pair", "virt", None), P("virt", "pair", None), P("pair", None, None), P("pair"))
    out_specs = P("pair", None, "virt")
    return jax.shard_map(body, mesh=mesh, in_specs=in_specs, out_specs=out_specs, check_vma=False)
```

```python
import functools

import jax
import jax.numpy as jnp
from jax import lax
from jax.experimental import pallas as pl
from jax.experimental.pallas import tpu as pltpu
from jax.sharding import PartitionSpec as P

MESH = pl.DeviceIdType.MESH
NX, NY, NZ = 4, 4, 8
PAIRS_DEV, VW, TILE = 4, 512, 64
ROWS = VW // NX
PART_A = ((0, 1), (0, 2))
PART_B = (((1, 1, 0, 8), (2, 1, 0, 4)), ((2, 1, 0, 8),))
PART_C = (((3, 1, 0, 8), (2, 1, 4, 4)), ((3, 1, 0, 8),))
LINE = ((1, 3), (2, 2))
QUADS = (3, 2)
F32, BF16 = jnp.float32, jnp.bfloat16


def dot_t(a, b):
    return lax.dot_general(a, b, (((1,), (1,)), ((), ())), preferred_element_type=F32)


class Slots:
    def __init__(self):
        self.names = {}

    def __getitem__(self, name):
        return self.names.setdefault(name, len(self.names))


def kernel(slots, sends, amp_hbm, pan_hbm, dom_hbm, mir_hbm, out_ref,
           amp_ref, pan_ref, dom_ref, mir_ref, stg, xbuf, pst, bb, tacc, trecv, sout, land_low, land_up,
           send_sem, recv_sem, loc_sem):
    x = lax.axis_index("virt")
    p = lax.axis_index("pair")
    c = p % 2
    z = (p // 2) % NZ
    y = p // (2 * NZ)
    half = y // 2
    ybase = y % 2

    xs = [(x + d) % NX for d in range(NX)]
    ys = [(y + d) % NY for d in range(NY)]
    zs = [(z + d) % NZ for d in range(NZ)]

    def dev(x_, y_, z_, c_):
        return ((y_ * NZ + z_) * 2 + c_, x_)

    def off(dx=0, dy=0, dz=0):
        return dev(xs[dx], ys[dy], zs[dz], c)

    sibling = dev(x, y, z, 1 - c)

    def copy(src, dst, name, device, group):
        return pltpu.make_async_remote_copy(
            src_ref=src, dst_ref=dst, send_sem=send_sem.at[sends[group]], recv_sem=recv_sem.at[slots[name]],
            device_id=device, device_id_type=MESH)

    def send(src, dst, name, device, group):
        copy(src, dst, name, device, group).start()

    def arrive(ref, name):
        pltpu.make_async_copy(ref, ref, recv_sem.at[slots[name]]).wait()

    def all_sent(ref, group):
        pltpu.make_async_copy(ref, ref, send_sem.at[sends[group]]).wait()

    def size(t=1, j=1, r=1, y_=1, z_=1):
        return bb.at[pl.ds(0, t), pl.ds(0, j), pl.ds(0, r), pl.ds(0, y_), pl.ds(0, z_)]

    loads = [pltpu.make_async_copy(src, dst, loc_sem.at[i]) for i, (src, dst) in enumerate(
        ((dom_hbm, dom_ref), (mir_hbm, mir_ref), (pan_hbm, pan_ref), (amp_hbm, amp_ref)))]
    for load in loads:
        load.start()

    barrier = pltpu.get_barrier_semaphore()
    peers = [off(dz=d) for d in range(1, NZ)]
    peers += [off(dx=dx, dy=dy) for dx in range(NX) for dy in (1, 3)]
    peers += [dev(xs[dx], ys[dy], z, (c, 1 - c)[dc])
              for dx in range(NX) for dy in (0, 2) for dc in range(2) if (dx, dy, dc) != (0, 0, 0)]
    for peer in peers:
        pl.semaphore_signal(barrier, inc=1, device_id=peer, device_id_type=MESH)

    tacc[...] = jnp.zeros_like(tacc)
    for load in loads:
        load.wait()

    lane = lax.broadcasted_iota(jnp.int32, (1, 128), 1)
    order = []
    for i in range(PAIRS_DEV):
        found = jnp.int32(0)
        for q in range(PAIRS_DEV):
            found = jnp.where(mir_ref[q] % PAIRS_DEV == i, jnp.int32(q), found)
        order.append(jnp.where(half == 0, jnp.int32(i), found))
    for i in range(PAIRS_DEV):
        for h in range(2):
            row = 2 * x + h
            parts = [jnp.where(lane < TILE, dom_ref[order[i], row, 2 * t], dom_ref[order[i], row, 2 * t + 1])
                     for t in range(4)]
            mask = jnp.concatenate(parts, axis=1).astype(F32)
            rows = pl.ds(h * TILE, TILE)
            stg[i, rows, :] = (amp_ref[order[i], rows, :].astype(F32) * mask).astype(BF16)

    def amp_slot(x_):
        return xbuf.at[half, pl.ds(pl.multiple_of(x_ * ROWS, ROWS), ROWS), :]

    def move(here, src, dst, name, device, group):
        @pl.when(jnp.logical_not(here))
        def _():
            pltpu.make_async_remote_copy(
                src_ref=src, dst_ref=dst, send_sem=send_sem.at[sends[group]], recv_sem=recv_sem.at[name],
                device_id=device, device_id_type=MESH).start()

        @pl.when(here)
        def _():
            pltpu.make_async_copy(src, dst, recv_sem.at[name]).start()

    def send_amp(i):
        move(jnp.logical_and(half == c, x == i), stg.at[i], amp_slot(x), slots[("amp", 0)] + x,
             dev(i, ybase + 2 * c, z, half), "amp")

    pl.semaphore_wait(barrier, len(peers))

    swap = copy(pan_ref.at[1 - c], pst, "swap", sibling, "swap")
    swap.start()
    swap.wait()
    mine = pan_ref[c].astype(F32)
    other = pst[...].astype(F32)
    first = jnp.where(c == 0, mine, other)
    second = jnp.where(c == 0, other, mine)
    for j in range(2):
        rows16 = jnp.concatenate([first[8 * j:8 * j + 8], second[8 * j:8 * j + 8]], axis=0).astype(BF16)
        for t in range(4):
            bb[t, j, 0, y, z] = rows16[:, 128 * t:128 * t + 128]

    def plane_a(j, r, y_):
        return bb.at[pl.ds(*PART_A[j]), j, r, y_, z]

    def send_plane(j):
        for dy in (0, 1, 3, 2):
            for dx in (0, 1, 3, 2):
                if (dx, dy) != (0, 0):
                    send(plane_a(j, 0, y), plane_a(j, -dx % NX, y), ("pa", j), off(dx=dx, dy=dy), "pa")

    def arrive_plane(j):
        arrive(size(t=PART_A[j][1], y_=3, z_=5), ("pa", j))

    def line_z(j, z_):
        return bb.at[pl.ds(*LINE[j]), j, 0, y, z_]

    def send_z(j):
        for d in (1, 7, 2, 6, 3, 5, 4):
            send(line_z(j, z), line_z(j, z), ("z1", j), off(dz=d), ("z1", j))

    def arrive_z(j):
        arrive(size(t=LINE[j][1], z_=7), ("z1", j))

    def line(box, j, r, y_):
        return bb.at[pl.ds(box[0], box[1]), j, r, y_, pl.ds(box[2], box[3])]

    def send_lines(j):
        for d in (1, 3, 2):
            for box in PART_B[j]:
                send(line(box, j, 0, y), line(box, j, -d % NX, y), ("lb", j), off(dx=d), ("li", j))
            for box in PART_C[j]:
                send(line(box, j, 0, y), line(box, j, 0, y), ("lc", j), off(dy=d), ("li", j))

    def arrive_lines_b(j):
        arrive(size(y_=3, r=QUADS[j], z_=4), ("lb", j))

    def arrive_lines_c(j):
        arrive(size(y_=3, r=QUADS[j], z_=4), ("lc", j))

    def ring_a(n, z_, part=None):
        r = pl.ds(2 * (n % 2), 2) if part is None else pl.ds(2 * (n % 2) + part, 1)
        return bb.at[pl.ds(*PART_A[n // 2]), n // 2, r, :, z_]

    def step_a(n, s):
        for way, sign, part in ((1, -1, 0), (7, 1, 1)):
            here = zs[sign * (s - 1)]
            if s > 1:
                arrive(ring_a(n, here), ("ra", n, way, s - 1))
            ref = ring_a(n, here, part if s == 4 else None)
            send(ref, ref, ("ra", n, way, s), off(dz=way), "ra")

    def ring_b(n, box, y_, part=None):
        r = pl.ds(2 * (n % 2), 2) if part is None else pl.ds(2 * (n % 2) + part, 1)
        return bb.at[pl.ds(box[0], box[1]), n // 2, r, y_, pl.ds(box[2], box[3])]

    def step_b(n, s):
        for d in (1, 3):
            if s > 1:
                arrive(size(r=2, y_=QUADS[n // 2], z_=4), ("rb", n, d, 1))
            for box in PART_B[n // 2]:
                ref = ring_b(n, box, y) if s == 1 else ring_b(n, box, ys[-d], d // 2)
                send(ref, ref, ("rb", n, d, s), off(dy=d), "rb")

    def ring_c(j, box, r, part=None):
        some = slice(None) if part is None else pl.ds(2 * part, 2)
        return bb.at[pl.ds(box[0], box[1]), j, r, some, pl.ds(box[2], box[3])]

    def step_c(j, s):
        for d in (1, 3):
            if s > 1:
                arrive(size(r=4, y_=QUADS[j], z_=4), ("rc", j, d, 1))
            for box in PART_C[j]:
                if s == 1:
                    send(ring_c(j, box, 0), ring_c(j, box, 4 - d), ("rc", j, d, 1), off(dx=d), "rc")
                else:
                    send(ring_c(j, box, 4 - d, d // 2), ring_c(j, box, 2, d // 2), ("rc", j, d, 2), off(dx=d), "rc")

    def ready(n):
        for part, way in ((0, 1), (1, 7)):
            arrive(ring_a(n, zs[4], part), ("ra", n, way, 4))
        for d in (1, 3):
            arrive(size(y_=QUADS[n // 2], z_=4), ("rb", n, d, 2))
        if n % 2 == 1:
            for d in (1, 3):
                arrive(size(r=2, y_=QUADS[n // 2], z_=4), ("rc", n // 2, d, 2))

    def amp_arrived(slot, x_):
        return xbuf.at[slot, pl.ds(x_ * ROWS, ROWS), :]

    def forward_amp():
        for x_ in range(NX):
            here = amp_arrived(c, x_)
            arrive(here, ("amp", x_))
            send(here, here, "fwd", sibling, "fwd")

    send_plane(0)
    send_z(0)
    send_plane(1)
    send_z(1)
    for i in range(PAIRS_DEV):
        send_amp(i)
    arrive_plane(0)
    step_a(0, 1)
    step_a(1, 1)
    arrive_z(0)
    send_lines(0)
    arrive_plane(1)
    step_a(2, 1)
    step_a(3, 1)
    arrive_z(1)
    send_lines(1)
    step_a(0, 2)
    step_a(1, 2)
    step_a(2, 2)
    arrive_lines_b(0)
    step_b(0, 1)
    step_b(1, 1)
    arrive_lines_c(0)
    step_c(0, 1)
    step_a(3, 2)
    forward_amp()
    step_a(0, 3)
    step_a(1, 3)
    arrive_lines_b(1)
    step_b(2, 1)
    step_b(3, 1)
    arrive_lines_c(1)
    step_c(1, 1)
    step_a(2, 3)
    step_a(3, 3)
    step_b(0, 2)
    step_a(0, 4)
    step_b(1, 2)
    step_a(1, 4)
    step_c(0, 2)
    arrive(xbuf.at[1 - c], "fwd")

    def between(n, part):
        if (n, part) == (0, 0):
            step_b(2, 2)
            step_a(2, 4)
            step_b(3, 2)
            step_c(1, 2)
            step_a(3, 4)

    def panel(j, r):
        return jnp.concatenate([bb[t, j, r].reshape(VW, 128) for t in range(4)], axis=1)

    def panel_half(j, r, h):
        return jnp.concatenate([bb[t, j, r, pl.ds(2 * h, 2)].reshape(VW // 2, 128) for t in range(4)], axis=1)

    for n in range(3):
        ready(n)

        both = [panel(n >> 1, 2 * (n & 1) + r) for r in range(2)]
        wide = jnp.concatenate(both, axis=1)
        done = jnp.concatenate([dot_t(xbuf[0], b).astype(BF16) for b in both], axis=0)
        tacc[...] += jnp.dot(wide, done, preferred_element_type=F32)

        between(n, 0)
        both = [panel(n >> 1, 2 * (n & 1) + r) for r in range(2)]
        wide = jnp.concatenate(both, axis=1)
        turned = jnp.concatenate([dot_t(b, xbuf[1]).astype(BF16) for b in both], axis=1)
        tacc[...] += dot_t(turned, wide)
        between(n, 1)

    ready(3)
    both = [panel(1, 2 + r) for r in range(2)]
    wide = jnp.concatenate(both, axis=1)
    done = jnp.concatenate([dot_t(xbuf[0], b).astype(BF16) for b in both], axis=0)

    def half_rows(h):
        part = [panel_half(1, 2 + r, h) for r in range(2)]
        turned = jnp.concatenate([dot_t(b, xbuf[1]).astype(BF16) for b in part], axis=1)
        rows = pl.ds(pl.multiple_of(h * 256, 256), 256)
        return rows, tacc[rows, :] + jnp.dot(jnp.concatenate(part, axis=1), done, preferred_element_type=F32) + dot_t(
            turned, wide)

    rows, value = half_rows(1 - c)
    tacc[rows, :] = value
    tswap = copy(tacc.at[rows, :], trecv, "tswap", sibling, "tswap")
    tswap.start()
    rows, value = half_rows(c)
    tacc[rows, :] = value
    tswap.wait()
    full = (tacc[rows, :] + trecv[...]).astype(BF16)
    for t in range(4):
        sout[t] = full[:, 128 * t:128 * t + 128]

    low_self = jnp.logical_and(half == 0, c == 0)
    up_self = jnp.logical_and(jnp.logical_and(half == 1, c == 1), x >= 2)
    got = slots[("out", 0)] + x
    rows = pl.ds(pl.multiple_of(c * 256, 256), 256)
    for t in range(NX):
        move(jnp.logical_and(low_self, x == t), sout.at[t], land_low.at[x, rows, :], got, dev(t, ybase, z, half), "low")
    for h in range(2):
        to = 2 * c + h
        move(jnp.logical_and(up_self, x == to), sout.at[:, pl.ds(128 * h, 128), :], land_up.at[x], got,
             dev(to, ybase + 2, z, half), "up")

    def mask_cols(i):
        return [jnp.where(lane < TILE, dom_ref[i, r, 2 * x], dom_ref[i, r, 2 * x + 1]).astype(F32) for r in range(8)]

    all_sent(size(r=3, y_=3, z_=5), "pa")
    for j in range(2):
        all_sent(size(t=LINE[j][1], z_=7), ("z1", j))
        all_sent(size(j=2, r=3, y_=QUADS[j], z_=4), ("li", j))
    all_sent(size(t=3, r=4, y_=4, z_=7), "ra")
    all_sent(size(t=3, r=4, y_=4, z_=5), "rb")
    all_sent(size(t=3, r=4, y_=4, z_=5), "rc")
    all_sent(xbuf.at[c], "fwd")

    for i in range(PAIRS_DEV):
        arrive(land_up.at[i], ("out", i))

    @pl.when(half == 0)
    def _():
        for i in range(PAIRS_DEV):
            masks = mask_cols(i)
            for r in range(8):
                rows_ = pl.ds(r * TILE, TILE)
                out_ref[i, rows_, :] = (land_low[i, rows_, :].astype(F32) * masks[r]).astype(BF16)

    @pl.when(half == 1)
    def _():
        for i in range(PAIRS_DEV):
            masks = mask_cols(i)
            block = land_up[mir_ref[i] % PAIRS_DEV].astype(F32)
            for t in range(4):
                turned = block[t].T
                for h in range(2):
                    out_ref[i, pl.ds(128 * t + TILE * h, TILE), :] = (
                        turned[TILE * h:TILE * h + TILE] * masks[2 * t + h]).astype(BF16)

    def most_sent(short, whole, less, group):
        @pl.when(short)
        def _():
            all_sent(less, group)

        @pl.when(jnp.logical_not(short))
        def _():
            all_sent(whole, group)

    most_sent(half == c, stg, stg.at[pl.ds(0, 3)], "amp")
    most_sent(low_self, sout, sout.at[pl.ds(0, 3)], "low")
    most_sent(up_self, sout, sout.at[pl.ds(0, 2)], "up")


def body(amplitudes, panels, domain, mirror):
    slots, sends = Slots(), Slots()
    for i in range(NX):
        slots[("amp", i)]
    for i in range(NX):
        slots[("out", i)]
    vm = pl.BlockSpec(memory_space=pltpu.VMEM)
    hbm = pl.BlockSpec(memory_space=pltpu.HBM)
    return pl.pallas_call(
        functools.partial(kernel, slots, sends),
        out_shape=jax.ShapeDtypeStruct((PAIRS_DEV, VW, ROWS), BF16),
        in_specs=[hbm] * 4,
        out_specs=vm,
        scratch_shapes=[
            pltpu.VMEM((PAIRS_DEV, ROWS, VW), BF16),
            pltpu.VMEM((2, 16, VW), BF16),
            pltpu.SMEM((PAIRS_DEV, 8, 8), jnp.int32),
            pltpu.SMEM((PAIRS_DEV,), jnp.int32),
            pltpu.VMEM((PAIRS_DEV, ROWS, VW), BF16),
            pltpu.VMEM((2, VW, VW), BF16),
            pltpu.VMEM((16, VW), BF16),
            pltpu.VMEM((4, 2, NX, NY, NZ, 16, 128), BF16),
            pltpu.VMEM((VW, VW), F32),
            pltpu.VMEM((256, VW), F32),
            pltpu.VMEM((4, 256, 128), BF16),
            pltpu.VMEM((PAIRS_DEV, VW, ROWS), BF16),
            pltpu.VMEM((PAIRS_DEV, 4, 128, 128), BF16),
            pltpu.SemaphoreType.DMA((14,)),
            pltpu.SemaphoreType.DMA((75,)),
            pltpu.SemaphoreType.DMA((4,)),
        ],
        name="ladder",
        cost_estimate=pl.CostEstimate(flops=8 * 2**30, bytes_accessed=2 * 2**20, transcendentals=0),
        compiler_params=pltpu.CompilerParams(collective_id=0, has_side_effects=True, vmem_limit_bytes=56 * 2**20),
    )(amplitudes, panels.reshape(2, 16, VW), domain, mirror).astype(F32)


def solution(mesh):
    in_specs = (P("pair", "virt", None), P("virt", "pair", None), P("pair", None, None), P("pair"))
    out_specs = P("pair", None, "virt")
    return jax.shard_map(body, mesh=mesh, in_specs=in_specs, out_specs=out_specs, check_vma=False)
```

```python
import functools

import jax
import jax.numpy as jnp
from jax import lax
from jax.experimental import pallas as pl
from jax.experimental.pallas import tpu as pltpu
from jax.sharding import PartitionSpec as P

MESH = pl.DeviceIdType.MESH
NX, NY, NZ = 4, 4, 8
PAIRS_DEV, VW, TILE = 4, 512, 64
ROWS = VW // NX
PART_A = ((0, 1), (0, 2))
PART_B = (((1, 1, 0, 8), (2, 1, 0, 4)), ((2, 1, 0, 8),))
PART_C = (((3, 1, 0, 8), (2, 1, 4, 4)), ((3, 1, 0, 8),))
LINE = ((1, 3), (2, 2))
QUADS = (3, 2)
F32, BF16 = jnp.float32, jnp.bfloat16


def dot_t(a, b):
    return lax.dot_general(a, b, (((1,), (1,)), ((), ())), preferred_element_type=F32)


class Slots:
    def __init__(self):
        self.names = {}

    def __getitem__(self, name):
        return self.names.setdefault(name, len(self.names))


def kernel(slots, sends, amp_hbm, pan_hbm, dom_hbm, mir_hbm, out_ref,
           amp_ref, pan_ref, dom_ref, mir_ref, stg, xbuf, pst, bb, tacc, trecv, sout, land_low, land_up,
           send_sem, recv_sem, loc_sem):
    x = lax.axis_index("virt")
    p = lax.axis_index("pair")
    c = p % 2
    z = (p // 2) % NZ
    y = p // (2 * NZ)
    half = y // 2
    ybase = y % 2

    xs = [(x + d) % NX for d in range(NX)]
    ys = [(y + d) % NY for d in range(NY)]
    zs = [(z + d) % NZ for d in range(NZ)]

    def dev(x_, y_, z_, c_):
        return ((y_ * NZ + z_) * 2 + c_, x_)

    def off(dx=0, dy=0, dz=0):
        return dev(xs[dx], ys[dy], zs[dz], c)

    sibling = dev(x, y, z, 1 - c)

    def copy(src, dst, name, device, group):
        return pltpu.make_async_remote_copy(
            src_ref=src, dst_ref=dst, send_sem=send_sem.at[sends[group]], recv_sem=recv_sem.at[slots[name]],
            device_id=device, device_id_type=MESH)

    def send(src, dst, name, device, group):
        copy(src, dst, name, device, group).start()

    def arrive(ref, name):
        pltpu.make_async_copy(ref, ref, recv_sem.at[slots[name]]).wait()

    def all_sent(ref, group):
        pltpu.make_async_copy(ref, ref, send_sem.at[sends[group]]).wait()

    def size(t=1, j=1, r=1, y_=1, z_=1):
        return bb.at[pl.ds(0, t), pl.ds(0, j), pl.ds(0, r), pl.ds(0, y_), pl.ds(0, z_)]

    loads = [pltpu.make_async_copy(src, dst, loc_sem.at[i]) for i, (src, dst) in enumerate(
        ((dom_hbm, dom_ref), (mir_hbm, mir_ref), (pan_hbm, pan_ref), (amp_hbm, amp_ref)))]
    for load in loads:
        load.start()

    barrier = pltpu.get_barrier_semaphore()
    peers = [off(dz=d) for d in range(1, NZ)]
    peers += [off(dx=dx, dy=dy) for dx in range(NX) for dy in (1, 3)]
    peers += [dev(xs[dx], ys[dy], z, (c, 1 - c)[dc])
              for dx in range(NX) for dy in (0, 2) for dc in range(2) if (dx, dy, dc) != (0, 0, 0)]
    for peer in peers:
        pl.semaphore_signal(barrier, inc=1, device_id=peer, device_id_type=MESH)

    tacc[...] = jnp.zeros_like(tacc)
    for load in loads:
        load.wait()

    lane = lax.broadcasted_iota(jnp.int32, (1, 128), 1)
    order = []
    for i in range(PAIRS_DEV):
        found = jnp.int32(0)
        for q in range(PAIRS_DEV):
            found = jnp.where(mir_ref[q] % PAIRS_DEV == i, jnp.int32(q), found)
        order.append(jnp.where(half == 0, jnp.int32(i), found))
    for i in range(PAIRS_DEV):
        for h in range(2):
            row = 2 * x + h
            parts = [jnp.where(lane < TILE, dom_ref[order[i], row, 2 * t], dom_ref[order[i], row, 2 * t + 1])
                     for t in range(4)]
            mask = jnp.concatenate(parts, axis=1).astype(F32)
            rows = pl.ds(h * TILE, TILE)
            stg[i, rows, :] = (amp_ref[order[i], rows, :].astype(F32) * mask).astype(BF16)

    def amp_slot(x_):
        return xbuf.at[half, pl.ds(pl.multiple_of(x_ * ROWS, ROWS), ROWS), :]

    def move(here, src, dst, name, device, group):
        @pl.when(jnp.logical_not(here))
        def _():
            pltpu.make_async_remote_copy(
                src_ref=src, dst_ref=dst, send_sem=send_sem.at[sends[group]], recv_sem=recv_sem.at[name],
                device_id=device, device_id_type=MESH).start()

        @pl.when(here)
        def _():
            pltpu.make_async_copy(src, dst, recv_sem.at[name]).start()

    def send_amp(i):
        move(jnp.logical_and(half == c, x == i), stg.at[i], amp_slot(x), slots[("amp", 0)] + x,
             dev(i, ybase + 2 * c, z, half), "amp")

    pl.semaphore_wait(barrier, len(peers))

    swap = copy(pan_ref.at[1 - c], pst, "swap", sibling, "swap")
    swap.start()
    swap.wait()
    mine = pan_ref[c].astype(F32)
    other = pst[...].astype(F32)
    first = jnp.where(c == 0, mine, other)
    second = jnp.where(c == 0, other, mine)
    for j in range(2):
        rows16 = jnp.concatenate([first[8 * j:8 * j + 8], second[8 * j:8 * j + 8]], axis=0).astype(BF16)
        for t in range(4):
            bb[t, j, 0, y, z] = rows16[:, 128 * t:128 * t + 128]

    def plane_a(j, r, y_):
        return bb.at[pl.ds(*PART_A[j]), j, r, y_, z]

    def send_plane(j):
        for dy in (0, 1, 3, 2):
            for dx in (0, 1, 3, 2):
                if (dx, dy) != (0, 0):
                    send(plane_a(j, 0, y), plane_a(j, -dx % NX, y), ("pa", j), off(dx=dx, dy=dy), "pa")

    def arrive_plane(j):
        arrive(size(t=PART_A[j][1], y_=3, z_=5), ("pa", j))

    def line_z(j, z_):
        return bb.at[pl.ds(*LINE[j]), j, 0, y, z_]

    def send_z(j):
        for d in (1, 7, 2, 6, 3, 5, 4):
            send(line_z(j, z), line_z(j, z), ("z1", j), off(dz=d), ("z1", j))

    def arrive_z(j):
        arrive(size(t=LINE[j][1], z_=7), ("z1", j))

    def line(box, j, r, y_):
        return bb.at[pl.ds(box[0], box[1]), j, r, y_, pl.ds(box[2], box[3])]

    def send_lines(j):
        for d in (1, 3, 2):
            for box in PART_B[j]:
                send(line(box, j, 0, y), line(box, j, -d % NX, y), ("lb", j), off(dx=d), ("li", j))
            for box in PART_C[j]:
                send(line(box, j, 0, y), line(box, j, 0, y), ("lc", j), off(dy=d), ("li", j))

    def arrive_lines_b(j):
        arrive(size(y_=3, r=QUADS[j], z_=4), ("lb", j))

    def arrive_lines_c(j):
        arrive(size(y_=3, r=QUADS[j], z_=4), ("lc", j))

    def ring_a(n, z_, part=None):
        r = pl.ds(2 * (n % 2), 2) if part is None else pl.ds(2 * (n % 2) + part, 1)
        return bb.at[pl.ds(*PART_A[n // 2]), n // 2, r, :, z_]

    def step_a(n, s):
        for way, sign, part in ((1, -1, 0), (7, 1, 1)):
            here = zs[sign * (s - 1)]
            if s > 1:
                arrive(ring_a(n, here), ("ra", n, way, s - 1))
            ref = ring_a(n, here, part if s == 4 else None)
            send(ref, ref, ("ra", n, way, s), off(dz=way), "ra")

    def ring_b(n, box, y_, part=None):
        r = pl.ds(2 * (n % 2), 2) if part is None else pl.ds(2 * (n % 2) + part, 1)
        return bb.at[pl.ds(box[0], box[1]), n // 2, r, y_, pl.ds(box[2], box[3])]

    def step_b(n, s):
        for d in (1, 3):
            if s > 1:
                arrive(size(r=2, y_=QUADS[n // 2], z_=4), ("rb", n, d, 1))
            for box in PART_B[n // 2]:
                ref = ring_b(n, box, y) if s == 1 else ring_b(n, box, ys[-d], d // 2)
                send(ref, ref, ("rb", n, d, s), off(dy=d), "rb")

    def ring_c(j, box, r, part=None):
        some = slice(None) if part is None else pl.ds(2 * part, 2)
        return bb.at[pl.ds(box[0], box[1]), j, r, some, pl.ds(box[2], box[3])]

    def step_c(j, s):
        for d in (1, 3):
            if s > 1:
                arrive(size(r=4, y_=QUADS[j], z_=4), ("rc", j, d, 1))
            for box in PART_C[j]:
                if s == 1:
                    send(ring_c(j, box, 0), ring_c(j, box, 4 - d), ("rc", j, d, 1), off(dx=d), "rc")
                else:
                    send(ring_c(j, box, 4 - d, d // 2), ring_c(j, box, 2, d // 2), ("rc", j, d, 2), off(dx=d), "rc")

    def ready(n):
        for part, way in ((0, 1), (1, 7)):
            arrive(ring_a(n, zs[4], part), ("ra", n, way, 4))
        for d in (1, 3):
            arrive(size(y_=QUADS[n // 2], z_=4), ("rb", n, d, 2))
        if n % 2 == 1:
            for d in (1, 3):
                arrive(size(r=2, y_=QUADS[n // 2], z_=4), ("rc", n // 2, d, 2))

    def amp_arrived(slot, x_):
        return xbuf.at[slot, pl.ds(x_ * ROWS, ROWS), :]

    def forward_amp():
        for x_ in range(NX):
            here = amp_arrived(c, x_)
            arrive(here, ("amp", x_))
            send(here, here, "fwd", sibling, "fwd")

    send_plane(0)
    send_z(0)
    send_plane(1)
    send_z(1)
    for i in range(PAIRS_DEV):
        send_amp(i)
    arrive_plane(0)
    step_a(0, 1)
    step_a(1, 1)
    arrive_z(0)
    send_lines(0)
    arrive_plane(1)
    step_a(2, 1)
    step_a(3, 1)
    arrive_z(1)
    send_lines(1)
    step_a(0, 2)
    step_a(1, 2)
    step_a(2, 2)
    arrive_lines_b(0)
    step_b(0, 1)
    step_b(1, 1)
    arrive_lines_c(0)
    step_c(0, 1)
    step_a(3, 2)
    forward_amp()
    step_a(0, 3)
    step_a(1, 3)
    arrive_lines_b(1)
    step_b(2, 1)
    step_b(3, 1)
    arrive_lines_c(1)
    step_c(1, 1)
    step_a(2, 3)
    step_a(3, 3)
    step_b(0, 2)
    step_a(0, 4)
    step_b(1, 2)
    step_a(1, 4)
    step_c(0, 2)
    arrive(xbuf.at[1 - c], "fwd")

    def between(n, part):
        if (n, part) == (0, 0):
            step_b(2, 2)
            step_a(2, 4)
            step_b(3, 2)
            step_c(1, 2)
            step_a(3, 4)

    def panel(j, r):
        return jnp.concatenate([bb[t, j, r].reshape(VW, 128) for t in range(4)], axis=1)

    def panel_half(j, r, h):
        return jnp.concatenate([bb[t, j, r, pl.ds(2 * h, 2)].reshape(VW // 2, 128) for t in range(4)], axis=1)

    for n in range(3):
        ready(n)

        both = [panel(n >> 1, 2 * (n & 1) + r) for r in range(2)]
        wide = jnp.concatenate(both, axis=1)
        done = jnp.concatenate([dot_t(xbuf[0], b).astype(BF16) for b in both], axis=0)
        tacc[...] += jnp.dot(wide, done, preferred_element_type=F32)

        between(n, 0)
        both = [panel(n >> 1, 2 * (n & 1) + r) for r in range(2)]
        wide = jnp.concatenate(both, axis=1)
        turned = jnp.concatenate([dot_t(b, xbuf[1]).astype(BF16) for b in both], axis=1)
        tacc[...] += dot_t(turned, wide)
        between(n, 1)

    ready(3)
    both = [panel(1, 2 + r) for r in range(2)]
    wide = jnp.concatenate(both, axis=1)
    done = jnp.concatenate([dot_t(xbuf[0], b).astype(BF16) for b in both], axis=0)

    def half_rows(h):
        part = [panel_half(1, 2 + r, h) for r in range(2)]
        turned = jnp.concatenate([dot_t(b, xbuf[1]).astype(BF16) for b in part], axis=1)
        rows = pl.ds(pl.multiple_of(h * 256, 256), 256)
        return rows, tacc[rows, :] + jnp.dot(jnp.concatenate(part, axis=1), done, preferred_element_type=F32) + dot_t(
            turned, wide)

    rows, value = half_rows(1 - c)
    tacc[rows, :] = value
    tswap = copy(tacc.at[rows, :], trecv, "tswap", sibling, "tswap")
    tswap.start()
    rows, value = half_rows(c)
    tacc[rows, :] = value
    tswap.wait()
    full = (tacc[rows, :] + trecv[...]).astype(BF16)
    for t in range(4):
        sout[t] = full[:, 128 * t:128 * t + 128]

    low_self = jnp.logical_and(half == 0, c == 0)
    up_self = jnp.logical_and(jnp.logical_and(half == 1, c == 1), x >= 2)
    got = slots[("out", 0)] + x
    rows = pl.ds(pl.multiple_of(c * 256, 256), 256)
    for t in range(NX):
        move(jnp.logical_and(low_self, x == t), sout.at[t], land_low.at[x, rows, :], got, dev(t, ybase, z, half), "low")
    for h in range(2):
        to = 2 * c + h
        move(jnp.logical_and(up_self, x == to), sout.at[:, pl.ds(128 * h, 128), :], land_up.at[x], got,
             dev(to, ybase + 2, z, half), "up")

    def mask_cols(i):
        return [jnp.where(lane < TILE, dom_ref[i, r, 2 * x], dom_ref[i, r, 2 * x + 1]).astype(F32) for r in range(8)]

    all_sent(size(r=3, y_=3, z_=5), "pa")
    for j in range(2):
        all_sent(size(t=LINE[j][1], z_=7), ("z1", j))
        all_sent(size(j=2, r=3, y_=QUADS[j], z_=4), ("li", j))
    all_sent(size(t=3, r=4, y_=4, z_=7), "ra")
    all_sent(size(t=3, r=4, y_=4, z_=5), "rb")
    all_sent(size(t=3, r=4, y_=4, z_=5), "rc")
    all_sent(xbuf.at[c], "fwd")

    for i in range(PAIRS_DEV):
        arrive(land_up.at[i], ("out", i))

    @pl.when(half == 0)
    def _():
        for i in range(PAIRS_DEV):
            masks = mask_cols(i)
            for r in range(8):
                rows_ = pl.ds(r * TILE, TILE)
                out_ref[i, rows_, :] = (land_low[i, rows_, :].astype(F32) * masks[r]).astype(BF16)

    @pl.when(half == 1)
    def _():
        for i in range(PAIRS_DEV):
            masks = mask_cols(i)
            block = land_up[mir_ref[i] % PAIRS_DEV].astype(F32)
            for t in range(4):
                turned = block[t].T
                for h in range(2):
                    out_ref[i, pl.ds(128 * t + TILE * h, TILE), :] = (
                        turned[TILE * h:TILE * h + TILE] * masks[2 * t + h]).astype(BF16)

    def most_sent(short, whole, less, group):
        @pl.when(short)
        def _():
            all_sent(less, group)

        @pl.when(jnp.logical_not(short))
        def _():
            all_sent(whole, group)

    most_sent(half == c, stg, stg.at[pl.ds(0, 3)], "amp")
    most_sent(low_self, sout, sout.at[pl.ds(0, 3)], "low")
    most_sent(up_self, sout, sout.at[pl.ds(0, 2)], "up")


def body(amplitudes, panels, domain, mirror):
    slots, sends = Slots(), Slots()
    for i in range(NX):
        slots[("amp", i)]
    for i in range(NX):
        slots[("out", i)]
    vm = pl.BlockSpec(memory_space=pltpu.VMEM)
    hbm = pl.BlockSpec(memory_space=pltpu.HBM)
    return pl.pallas_call(
        functools.partial(kernel, slots, sends),
        out_shape=jax.ShapeDtypeStruct((PAIRS_DEV, VW, ROWS), BF16),
        in_specs=[hbm] * 4,
        out_specs=vm,
        scratch_shapes=[
            pltpu.VMEM((PAIRS_DEV, ROWS, VW), BF16),
            pltpu.VMEM((2, 16, VW), BF16),
            pltpu.SMEM((PAIRS_DEV, 8, 8), jnp.int32),
            pltpu.SMEM((PAIRS_DEV,), jnp.int32),
            pltpu.VMEM((PAIRS_DEV, ROWS, VW), BF16),
            pltpu.VMEM((2, VW, VW), BF16),
            pltpu.VMEM((16, VW), BF16),
            pltpu.VMEM((4, 2, NX, NY, NZ, 16, 128), BF16),
            pltpu.VMEM((VW, VW), F32),
            pltpu.VMEM((256, VW), F32),
            pltpu.VMEM((4, 256, 128), BF16),
            pltpu.VMEM((PAIRS_DEV, VW, ROWS), BF16),
            pltpu.VMEM((PAIRS_DEV, 4, 128, 128), BF16),
            pltpu.SemaphoreType.DMA((14,)),
            pltpu.SemaphoreType.DMA((75,)),
            pltpu.SemaphoreType.DMA((4,)),
        ],
        name="ladder",
        cost_estimate=pl.CostEstimate(flops=8 * 2**30, bytes_accessed=2 * 2**20, transcendentals=0),
        compiler_params=pltpu.CompilerParams(collective_id=0, has_side_effects=True, vmem_limit_bytes=48 * 2**20),
    )(*(pltpu.with_memory_space_constraint(a, pltpu.HBM) for a in (amplitudes, panels.reshape(2, 16, VW), domain, mirror))).astype(F32)


def solution(mesh):
    in_specs = (P("pair", "virt", None), P("virt", "pair", None), P("pair", None, None), P("pair"))
    out_specs = P("pair", None, "virt")
    return jax.shard_map(body, mesh=mesh, in_specs=in_specs, out_specs=out_specs, check_vma=False)
```

```python
import functools

import jax
import jax.numpy as jnp
from jax import lax
from jax.experimental import pallas as pl
from jax.experimental.pallas import tpu as pltpu
from jax.sharding import PartitionSpec as P

MESH = pl.DeviceIdType.MESH
NX, NY, NZ = 4, 4, 8
PAIRS_DEV, VW, TILE = 4, 512, 64
ROWS = VW // NX
PART_A = ((0, 1), (0, 2))
PART_B = (((1, 1, 0, 8), (2, 1, 0, 4)), ((2, 1, 0, 8),))
PART_C = (((3, 1, 0, 8), (2, 1, 4, 4)), ((3, 1, 0, 8),))
LINE = ((1, 3), (2, 2))
QUADS = (3, 2)
F32, BF16 = jnp.float32, jnp.bfloat16


def dot_t(a, b):
    return lax.dot_general(a, b, (((1,), (1,)), ((), ())), preferred_element_type=F32)


class Slots:
    def __init__(self):
        self.names = {}

    def __getitem__(self, name):
        return self.names.setdefault(name, len(self.names))


def kernel(slots, sends, amp_hbm, pan_hbm, dom_hbm, mir_hbm, out_ref,
           amp_ref, pan_ref, dom_ref, mir_ref, stg, xbuf, pst, bb, tacc, trecv, dn, sout, land_low, land_up,
           send_sem, recv_sem, loc_sem):
    x = lax.axis_index("virt")
    p = lax.axis_index("pair")
    c = p % 2
    z = (p // 2) % NZ
    y = p // (2 * NZ)
    half = y // 2
    ybase = y % 2

    xs = [(x + d) % NX for d in range(NX)]
    ys = [(y + d) % NY for d in range(NY)]
    zs = [(z + d) % NZ for d in range(NZ)]

    def dev(x_, y_, z_, c_):
        return ((y_ * NZ + z_) * 2 + c_, x_)

    def off(dx=0, dy=0, dz=0):
        return dev(xs[dx], ys[dy], zs[dz], c)

    sibling = dev(x, y, z, 1 - c)

    def copy(src, dst, name, device, group):
        return pltpu.make_async_remote_copy(
            src_ref=src, dst_ref=dst, send_sem=send_sem.at[sends[group]], recv_sem=recv_sem.at[slots[name]],
            device_id=device, device_id_type=MESH)

    def send(src, dst, name, device, group):
        copy(src, dst, name, device, group).start()

    def arrive(ref, name):
        pltpu.make_async_copy(ref, ref, recv_sem.at[slots[name]]).wait()

    def all_sent(ref, group):
        pltpu.make_async_copy(ref, ref, send_sem.at[sends[group]]).wait()

    def size(t=1, j=1, r=1, y_=1, z_=1):
        return bb.at[pl.ds(0, t), pl.ds(0, j), pl.ds(0, r), pl.ds(0, y_), pl.ds(0, z_)]

    loads = [pltpu.make_async_copy(src, dst, loc_sem.at[i]) for i, (src, dst) in enumerate(
        ((dom_hbm, dom_ref), (mir_hbm, mir_ref), (pan_hbm, pan_ref), (amp_hbm, amp_ref)))]
    for load in loads:
        load.start()

    barrier = pltpu.get_barrier_semaphore()
    peers = [off(dz=d) for d in range(1, NZ)]
    peers += [off(dx=dx, dy=dy) for dx in range(NX) for dy in (1, 3)]
    peers += [dev(xs[dx], ys[dy], z, (c, 1 - c)[dc])
              for dx in range(NX) for dy in (0, 2) for dc in range(2) if (dx, dy, dc) != (0, 0, 0)]
    for peer in peers:
        pl.semaphore_signal(barrier, inc=1, device_id=peer, device_id_type=MESH)

    tacc[...] = jnp.zeros_like(tacc)
    for load in loads:
        load.wait()

    lane = lax.broadcasted_iota(jnp.int32, (1, 128), 1)
    order = []
    for i in range(PAIRS_DEV):
        found = jnp.int32(0)
        for q in range(PAIRS_DEV):
            found = jnp.where(mir_ref[q] % PAIRS_DEV == i, jnp.int32(q), found)
        order.append(jnp.where(half == 0, jnp.int32(i), found))
    for i in range(PAIRS_DEV):
        for h in range(2):
            row = 2 * x + h
            parts = [jnp.where(lane < TILE, dom_ref[order[i], row, 2 * t], dom_ref[order[i], row, 2 * t + 1])
                     for t in range(4)]
            mask = jnp.concatenate(parts, axis=1).astype(F32)
            rows = pl.ds(h * TILE, TILE)
            stg[i, rows, :] = (amp_ref[order[i], rows, :].astype(F32) * mask).astype(BF16)

    def amp_slot(x_):
        return xbuf.at[half, pl.ds(pl.multiple_of(x_ * ROWS, ROWS), ROWS), :]

    def move(here, src, dst, name, device, group):
        @pl.when(jnp.logical_not(here))
        def _():
            pltpu.make_async_remote_copy(
                src_ref=src, dst_ref=dst, send_sem=send_sem.at[sends[group]], recv_sem=recv_sem.at[name],
                device_id=device, device_id_type=MESH).start()

        @pl.when(here)
        def _():
            pltpu.make_async_copy(src, dst, recv_sem.at[name]).start()

    def send_amp(d):
        i = xs[d]
        move(jnp.logical_and(half == c, d == 0), stg.at[i], amp_slot(x), slots[("amp", 0)] + x,
             dev(i, ybase + 2 * c, z, half), "amp")

    pl.semaphore_wait(barrier, len(peers))

    swap = copy(pan_ref.at[1 - c], pst, "swap", sibling, "swap")
    swap.start()
    swap.wait()
    mine = pan_ref[c].astype(F32)
    other = pst[...].astype(F32)
    first = jnp.where(c == 0, mine, other)
    second = jnp.where(c == 0, other, mine)
    for j in range(2):
        rows16 = jnp.concatenate([first[8 * j:8 * j + 8], second[8 * j:8 * j + 8]], axis=0).astype(BF16)
        for t in range(4):
            bb[t, j, 0, y, z] = rows16[:, 128 * t:128 * t + 128]

    def plane_a(j, r, y_):
        return bb.at[pl.ds(*PART_A[j]), j, r, y_, z]

    def send_plane(j):
        for dy in (0, 1, 3, 2):
            for dx in (0, 1, 3, 2):
                if (dx, dy) != (0, 0):
                    send(plane_a(j, 0, y), plane_a(j, -dx % NX, y), ("pa", j), off(dx=dx, dy=dy), "pa")

    def arrive_plane(j):
        arrive(size(t=PART_A[j][1], y_=3, z_=5), ("pa", j))

    def line_z(j, z_):
        return bb.at[pl.ds(*LINE[j]), j, 0, y, z_]

    def send_z(j):
        for d in (1, 7, 2, 6, 3, 5, 4):
            send(line_z(j, z), line_z(j, z), ("z1", j), off(dz=d), ("z1", j))

    def arrive_z(j):
        arrive(size(t=LINE[j][1], z_=7), ("z1", j))

    def line(box, j, r, y_):
        return bb.at[pl.ds(box[0], box[1]), j, r, y_, pl.ds(box[2], box[3])]

    def send_lines(j):
        for d in (1, 3, 2):
            for box in PART_B[j]:
                send(line(box, j, 0, y), line(box, j, -d % NX, y), ("lb", j), off(dx=d), ("li", j))
            for box in PART_C[j]:
                send(line(box, j, 0, y), line(box, j, 0, y), ("lc", j), off(dy=d), ("li", j))

    def arrive_lines_b(j):
        arrive(size(y_=3, r=QUADS[j], z_=4), ("lb", j))

    def arrive_lines_c(j):
        arrive(size(y_=3, r=QUADS[j], z_=4), ("lc", j))

    def ring_a(n, z_, part=None):
        r = pl.ds(2 * (n % 2), 2) if part is None else pl.ds(2 * (n % 2) + part, 1)
        return bb.at[pl.ds(*PART_A[n // 2]), n // 2, r, :, z_]

    def step_a(n, s):
        for way, sign, part in ((1, -1, 0), (7, 1, 1)):
            here = zs[sign * (s - 1)]
            if s > 1:
                arrive(ring_a(n, here), ("ra", n, way, s - 1))
            ref = ring_a(n, here, part if s == 4 else None)
            send(ref, ref, ("ra", n, way, s), off(dz=way), "ra")

    def ring_b(n, box, y_, part=None):
        r = pl.ds(2 * (n % 2), 2) if part is None else pl.ds(2 * (n % 2) + part, 1)
        return bb.at[pl.ds(box[0], box[1]), n // 2, r, y_, pl.ds(box[2], box[3])]

    def step_b(n, s):
        for d in (1, 3):
            if s > 1:
                arrive(size(r=2, y_=QUADS[n // 2], z_=4), ("rb", n, d, 1))
            for box in PART_B[n // 2]:
                ref = ring_b(n, box, y) if s == 1 else ring_b(n, box, ys[-d], d // 2)
                send(ref, ref, ("rb", n, d, s), off(dy=d), "rb")

    def ring_c(j, box, r, part=None):
        some = slice(None) if part is None else pl.ds(2 * part, 2)
        return bb.at[pl.ds(box[0], box[1]), j, r, some, pl.ds(box[2], box[3])]

    def step_c(j, s):
        for d in (1, 3):
            if s > 1:
                arrive(size(r=4, y_=QUADS[j], z_=4), ("rc", j, d, 1))
            for box in PART_C[j]:
                if s == 1:
                    send(ring_c(j, box, 0), ring_c(j, box, 4 - d), ("rc", j, d, 1), off(dx=d), "rc")
                else:
                    send(ring_c(j, box, 4 - d, d // 2), ring_c(j, box, 2, d // 2), ("rc", j, d, 2), off(dx=d), "rc")

    def ready(n):
        for part, way in ((0, 1), (1, 7)):
            arrive(ring_a(n, zs[4], part), ("ra", n, way, 4))
        for d in (1, 3):
            arrive(size(y_=QUADS[n // 2], z_=4), ("rb", n, d, 2))
        if n % 2 == 1:
            for d in (1, 3):
                arrive(size(r=2, y_=QUADS[n // 2], z_=4), ("rc", n // 2, d, 2))

    def amp_arrived(slot, x_):
        return xbuf.at[slot, pl.ds(x_ * ROWS, ROWS), :]

    def forward_amp():
        for x_ in range(NX):
            here = amp_arrived(c, x_)
            arrive(here, ("amp", x_))
            send(here, here, "fwd", sibling, "fwd")

    send_plane(0)
    send_z(0)
    send_plane(1)
    send_z(1)
    for d in (1, 3, 2, 0):
        send_amp(d)
    arrive_plane(0)
    step_a(0, 1)
    step_a(1, 1)
    arrive_z(0)
    send_lines(0)
    arrive_plane(1)
    step_a(2, 1)
    step_a(3, 1)
    arrive_z(1)
    send_lines(1)
    step_a(0, 2)
    step_a(1, 2)
    step_a(2, 2)
    arrive_lines_b(0)
    step_b(0, 1)
    step_b(1, 1)
    arrive_lines_c(0)
    step_c(0, 1)
    step_a(3, 2)
    forward_amp()
    step_a(0, 3)
    step_a(1, 3)
    arrive_lines_b(1)
    step_b(2, 1)
    step_b(3, 1)
    arrive_lines_c(1)
    step_c(1, 1)
    step_a(2, 3)
    step_a(3, 3)
    step_b(0, 2)
    step_a(0, 4)
    step_b(1, 2)
    step_a(1, 4)
    step_c(0, 2)
    arrive(xbuf.at[1 - c], "fwd")

    def between(n, part):
        if (n, part) == (0, 0):
            step_b(2, 2)
            step_a(2, 4)
            step_b(3, 2)
            step_c(1, 2)
            step_a(3, 4)

    def panel(j, r):
        return jnp.concatenate([bb[t, j, r].reshape(VW, 128) for t in range(4)], axis=1)

    def panel_half(j, r, h):
        return jnp.concatenate([bb[t, j, r, pl.ds(2 * h, 2)].reshape(VW // 2, 128) for t in range(4)], axis=1)

    def first_sum(n):
        both = [panel(n >> 1, 2 * (n & 1) + r) for r in range(2)]
        done = jnp.concatenate([dot_t(xbuf[0], b).astype(BF16) for b in both], axis=0)
        tacc[...] += jnp.dot(jnp.concatenate(both, axis=1), done, preferred_element_type=F32)

    for n in range(2):
        ready(n)
        first_sum(n)
        between(n, 0)
        both = [panel(n >> 1, 2 * (n & 1) + r) for r in range(2)]
        turned = jnp.concatenate([dot_t(b, xbuf[1]).astype(BF16) for b in both], axis=1)
        tacc[...] += dot_t(turned, jnp.concatenate(both, axis=1))
        between(n, 1)

    for n in (2, 3):
        ready(n)
        for r in range(2):
            dn[2 * (n - 2) + r] = dot_t(xbuf[0], panel(1, 2 * (n - 2) + r)).astype(BF16)

    def half_rows(h):
        rows = pl.ds(pl.multiple_of(h * 256, 256), 256)
        part = [panel_half(1, r, h) for r in range(NX)]
        turned = jnp.concatenate([dot_t(b, xbuf[1]).astype(BF16) for b in part], axis=1)
        tacc[rows, :] += jnp.dot(
            jnp.concatenate(part, axis=1), dn[...].reshape(NX * VW, VW), preferred_element_type=F32
        ) + dot_t(turned, jnp.concatenate([panel(1, r) for r in range(NX)], axis=1))
        return rows

    rows = half_rows(1 - c)
    tswap = copy(tacc.at[rows, :], trecv, "tswap", sibling, "tswap")
    tswap.start()
    rows = half_rows(c)
    tswap.wait()
    full = (tacc[rows, :] + trecv[...]).astype(BF16)
    for t in range(4):
        sout[t] = full[:, 128 * t:128 * t + 128]

    low_self = jnp.logical_and(half == 0, c == 0)
    up_self = jnp.logical_and(jnp.logical_and(half == 1, c == 1), x >= 2)
    got = slots[("out", 0)] + x
    rows = pl.ds(pl.multiple_of(c * 256, 256), 256)
    for d in (1, 3, 2, 0):
        t = xs[d]
        move(jnp.logical_and(low_self, d == 0), sout.at[t], land_low.at[x, rows, :], got, dev(t, ybase, z, half), "low")
    for h in range(2):
        to = 2 * c + h
        move(jnp.logical_and(up_self, x == to), sout.at[:, pl.ds(128 * h, 128), :], land_up.at[x], got,
             dev(to, ybase + 2, z, half), "up")

    def mask_cols(i):
        return [jnp.where(lane < TILE, dom_ref[i, r, 2 * x], dom_ref[i, r, 2 * x + 1]).astype(F32) for r in range(8)]

    all_sent(size(r=3, y_=3, z_=5), "pa")
    for j in range(2):
        all_sent(size(t=LINE[j][1], z_=7), ("z1", j))
        all_sent(size(j=2, r=3, y_=QUADS[j], z_=4), ("li", j))
    all_sent(size(t=3, r=4, y_=4, z_=7), "ra")
    all_sent(size(t=3, r=4, y_=4, z_=5), "rb")
    all_sent(size(t=3, r=4, y_=4, z_=5), "rc")
    all_sent(xbuf.at[c], "fwd")

    for i in range(PAIRS_DEV):
        arrive(land_up.at[i], ("out", i))

    @pl.when(half == 0)
    def _():
        for i in range(PAIRS_DEV):
            masks = mask_cols(i)
            for r in range(8):
                rows_ = pl.ds(r * TILE, TILE)
                out_ref[i, rows_, :] = (land_low[i, rows_, :].astype(F32) * masks[r]).astype(BF16)

    @pl.when(half == 1)
    def _():
        for i in range(PAIRS_DEV):
            masks = mask_cols(i)
            block = land_up[mir_ref[i] % PAIRS_DEV].astype(F32)
            for t in range(4):
                turned = block[t].T
                for h in range(2):
                    out_ref[i, pl.ds(128 * t + TILE * h, TILE), :] = (
                        turned[TILE * h:TILE * h + TILE] * masks[2 * t + h]).astype(BF16)

    def most_sent(short, whole, less, group):
        @pl.when(short)
        def _():
            all_sent(less, group)

        @pl.when(jnp.logical_not(short))
        def _():
            all_sent(whole, group)

    most_sent(half == c, stg, stg.at[pl.ds(0, 3)], "amp")
    most_sent(low_self, sout, sout.at[pl.ds(0, 3)], "low")
    most_sent(up_self, sout, sout.at[pl.ds(0, 2)], "up")


def body(amplitudes, panels, domain, mirror):
    slots, sends = Slots(), Slots()
    for i in range(NX):
        slots[("amp", i)]
    for i in range(NX):
        slots[("out", i)]
    vm = pl.BlockSpec(memory_space=pltpu.VMEM)
    hbm = pl.BlockSpec(memory_space=pltpu.HBM)
    return pl.pallas_call(
        functools.partial(kernel, slots, sends),
        out_shape=jax.ShapeDtypeStruct((PAIRS_DEV, VW, ROWS), BF16),
        in_specs=[hbm] * 4,
        out_specs=vm,
        scratch_shapes=[
            pltpu.VMEM((PAIRS_DEV, ROWS, VW), BF16),
            pltpu.VMEM((2, 16, VW), BF16),
            pltpu.SMEM((PAIRS_DEV, 8, 8), jnp.int32),
            pltpu.SMEM((PAIRS_DEV,), jnp.int32),
            pltpu.VMEM((PAIRS_DEV, ROWS, VW), BF16),
            pltpu.VMEM((2, VW, VW), BF16),
            pltpu.VMEM((16, VW), BF16),
            pltpu.VMEM((4, 2, NX, NY, NZ, 16, 128), BF16),
            pltpu.VMEM((VW, VW), F32),
            pltpu.VMEM((256, VW), F32),
            pltpu.VMEM((NX, VW, VW), BF16),
            pltpu.VMEM((4, 256, 128), BF16),
            pltpu.VMEM((PAIRS_DEV, VW, ROWS), BF16),
            pltpu.VMEM((PAIRS_DEV, 4, 128, 128), BF16),
            pltpu.SemaphoreType.DMA((14,)),
            pltpu.SemaphoreType.DMA((75,)),
            pltpu.SemaphoreType.DMA((4,)),
        ],
        name="ladder",
        cost_estimate=pl.CostEstimate(flops=8 * 2**30, bytes_accessed=2 * 2**20, transcendentals=0),
        compiler_params=pltpu.CompilerParams(collective_id=0, has_side_effects=True, vmem_limit_bytes=48 * 2**20),
    )(*(pltpu.with_memory_space_constraint(a, pltpu.HBM) for a in (amplitudes, panels.reshape(2, 16, VW), domain, mirror))).astype(F32)


def solution(mesh):
    in_specs = (P("pair", "virt", None), P("virt", "pair", None), P("pair", None, None), P("pair"))
    out_specs = P("pair", None, "virt")
    return jax.shard_map(body, mesh=mesh, in_specs=in_specs, out_specs=out_specs, check_vma=False)
```

```python
import functools

import jax
import jax.numpy as jnp
from jax import lax
from jax.experimental import pallas as pl
from jax.experimental.pallas import tpu as pltpu
from jax.sharding import PartitionSpec as P

MESH = pl.DeviceIdType.MESH
NX, NY, NZ = 4, 4, 8
PAIRS_DEV, VW, TILE = 4, 512, 64
ROWS = VW // NX
PART_A = ((0, 2), (0, 1))
PART_B = (((2, 1, 0, 8),), ((1, 1, 0, 8), (2, 1, 0, 4)))
PART_C = (((3, 1, 0, 8),), ((3, 1, 0, 8), (2, 1, 4, 4)))
LINE = ((2, 2), (1, 3))
QUADS = (2, 3)
F32, BF16 = jnp.float32, jnp.bfloat16


def dot_t(a, b):
    return lax.dot_general(a, b, (((1,), (1,)), ((), ())), preferred_element_type=F32)


class Slots:
    def __init__(self):
        self.names = {}

    def __getitem__(self, name):
        return self.names.setdefault(name, len(self.names))


def kernel(slots, sends, amp_hbm, pan_hbm, dom_hbm, mir_hbm, out_ref,
           amp_ref, pan_ref, dom_ref, mir_ref, stg, xbuf, pst, bb, tacc, trecv, dn, sout, land_low, land_up,
           send_sem, recv_sem, loc_sem):
    x = lax.axis_index("virt")
    p = lax.axis_index("pair")
    c = p % 2
    z = (p // 2) % NZ
    y = p // (2 * NZ)
    half = y // 2
    ybase = y % 2

    xs = [(x + d) % NX for d in range(NX)]
    ys = [(y + d) % NY for d in range(NY)]
    zs = [(z + d) % NZ for d in range(NZ)]

    def dev(x_, y_, z_, c_):
        return ((y_ * NZ + z_) * 2 + c_, x_)

    def off(dx=0, dy=0, dz=0):
        return dev(xs[dx], ys[dy], zs[dz], c)

    sibling = dev(x, y, z, 1 - c)

    def copy(src, dst, name, device, group):
        return pltpu.make_async_remote_copy(
            src_ref=src, dst_ref=dst, send_sem=send_sem.at[sends[group]], recv_sem=recv_sem.at[slots[name]],
            device_id=device, device_id_type=MESH)

    def send(src, dst, name, device, group):
        copy(src, dst, name, device, group).start()

    def arrive(ref, name):
        pltpu.make_async_copy(ref, ref, recv_sem.at[slots[name]]).wait()

    def all_sent(ref, group):
        pltpu.make_async_copy(ref, ref, send_sem.at[sends[group]]).wait()

    def size(t=1, j=1, r=1, y_=1, z_=1):
        return bb.at[pl.ds(0, t), pl.ds(0, j), pl.ds(0, r), pl.ds(0, y_), pl.ds(0, z_)]

    loads = [pltpu.make_async_copy(src, dst, loc_sem.at[i]) for i, (src, dst) in enumerate(
        ((dom_hbm, dom_ref), (mir_hbm, mir_ref), (pan_hbm, pan_ref), (amp_hbm, amp_ref)))]
    for load in loads:
        load.start()

    barrier = pltpu.get_barrier_semaphore()
    peers = [off(dz=d) for d in range(1, NZ)]
    peers += [off(dx=dx, dy=dy) for dx in range(NX) for dy in (1, 3)]
    peers += [dev(xs[dx], ys[dy], z, (c, 1 - c)[dc])
              for dx in range(NX) for dy in (0, 2) for dc in range(2) if (dx, dy, dc) != (0, 0, 0)]
    for peer in peers:
        pl.semaphore_signal(barrier, inc=1, device_id=peer, device_id_type=MESH)

    tacc[...] = jnp.zeros_like(tacc)
    for load in loads:
        load.wait()

    lane = lax.broadcasted_iota(jnp.int32, (1, 128), 1)
    order = []
    for i in range(PAIRS_DEV):
        found = jnp.int32(0)
        for q in range(PAIRS_DEV):
            found = jnp.where(mir_ref[q] % PAIRS_DEV == i, jnp.int32(q), found)
        order.append(jnp.where(half == 0, jnp.int32(i), found))
    for i in range(PAIRS_DEV):
        for h in range(2):
            row = 2 * x + h
            parts = [jnp.where(lane < TILE, dom_ref[order[i], row, 2 * t], dom_ref[order[i], row, 2 * t + 1])
                     for t in range(4)]
            mask = jnp.concatenate(parts, axis=1).astype(F32)
            rows = pl.ds(h * TILE, TILE)
            stg[i, rows, :] = (amp_ref[order[i], rows, :].astype(F32) * mask).astype(BF16)

    def amp_slot(x_):
        return xbuf.at[half, pl.ds(pl.multiple_of(x_ * ROWS, ROWS), ROWS), :]

    def move(here, src, dst, name, device, group):
        @pl.when(jnp.logical_not(here))
        def _():
            pltpu.make_async_remote_copy(
                src_ref=src, dst_ref=dst, send_sem=send_sem.at[sends[group]], recv_sem=recv_sem.at[name],
                device_id=device, device_id_type=MESH).start()

        @pl.when(here)
        def _():
            pltpu.make_async_copy(src, dst, recv_sem.at[name]).start()

    def send_amp(d):
        i = xs[d]
        move(jnp.logical_and(half == c, d == 0), stg.at[i], amp_slot(x), slots[("amp", 0)] + x,
             dev(i, ybase + 2 * c, z, half), "amp")

    pl.semaphore_wait(barrier, len(peers))

    swap = copy(pan_ref.at[1 - c], pst, "swap", sibling, "swap")
    swap.start()
    swap.wait()
    mine = pan_ref[c].astype(F32)
    other = pst[...].astype(F32)
    first = jnp.where(c == 0, mine, other)
    second = jnp.where(c == 0, other, mine)
    for j in range(2):
        rows16 = jnp.concatenate([first[8 * j:8 * j + 8], second[8 * j:8 * j + 8]], axis=0).astype(BF16)
        for t in range(4):
            bb[t, j, 0, y, z] = rows16[:, 128 * t:128 * t + 128]

    def plane_a(j, r, y_):
        return bb.at[pl.ds(*PART_A[j]), j, r, y_, z]

    def send_plane(j):
        for dy in (0, 1, 3, 2):
            for dx in (0, 1, 3, 2):
                if (dx, dy) != (0, 0):
                    send(plane_a(j, 0, y), plane_a(j, -dx % NX, y), ("pa", j), off(dx=dx, dy=dy), "pa")

    def arrive_plane(j):
        arrive(size(t=PART_A[j][1], y_=3, z_=5), ("pa", j))

    def line_z(j, z_):
        return bb.at[pl.ds(*LINE[j]), j, 0, y, z_]

    def send_z(j):
        for d in (1, 7, 2, 6, 3, 5, 4):
            send(line_z(j, z), line_z(j, z), ("z1", j), off(dz=d), ("z1", j))

    def arrive_z(j):
        arrive(size(t=LINE[j][1], z_=7), ("z1", j))

    def line(box, j, r, y_):
        return bb.at[pl.ds(box[0], box[1]), j, r, y_, pl.ds(box[2], box[3])]

    def send_lines(j):
        for d in (1, 3, 2):
            for box in PART_B[j]:
                send(line(box, j, 0, y), line(box, j, -d % NX, y), ("lb", j), off(dx=d), ("li", j))
            for box in PART_C[j]:
                send(line(box, j, 0, y), line(box, j, 0, y), ("lc", j), off(dy=d), ("li", j))

    def arrive_lines_b(j):
        arrive(size(y_=3, r=QUADS[j], z_=4), ("lb", j))

    def arrive_lines_c(j):
        arrive(size(y_=3, r=QUADS[j], z_=4), ("lc", j))

    def ring_a(n, z_, part=None):
        r = pl.ds(2 * (n % 2), 2) if part is None else pl.ds(2 * (n % 2) + part, 1)
        return bb.at[pl.ds(*PART_A[n // 2]), n // 2, r, :, z_]

    def step_a(n, s):
        for way, sign, part in ((1, -1, 0), (7, 1, 1)):
            here = zs[sign * (s - 1)]
            if s > 1:
                arrive(ring_a(n, here), ("ra", n, way, s - 1))
            ref = ring_a(n, here, part if s == 4 else None)
            send(ref, ref, ("ra", n, way, s), off(dz=way), "ra")

    def ring_b(n, box, y_, part=None):
        r = pl.ds(2 * (n % 2), 2) if part is None else pl.ds(2 * (n % 2) + part, 1)
        return bb.at[pl.ds(box[0], box[1]), n // 2, r, y_, pl.ds(box[2], box[3])]

    def step_b(n, s):
        for d in (1, 3):
            if s > 1:
                arrive(size(r=2, y_=QUADS[n // 2], z_=4), ("rb", n, d, 1))
            for box in PART_B[n // 2]:
                ref = ring_b(n, box, y) if s == 1 else ring_b(n, box, ys[-d], d // 2)
                send(ref, ref, ("rb", n, d, s), off(dy=d), "rb")

    def ring_c(j, box, r, part=None):
        some = slice(None) if part is None else pl.ds(2 * part, 2)
        return bb.at[pl.ds(box[0], box[1]), j, r, some, pl.ds(box[2], box[3])]

    def step_c(j, s):
        for d in (1, 3):
            if s > 1:
                arrive(size(r=4, y_=QUADS[j], z_=4), ("rc", j, d, 1))
            for box in PART_C[j]:
                if s == 1:
                    send(ring_c(j, box, 0), ring_c(j, box, 4 - d), ("rc", j, d, 1), off(dx=d), "rc")
                else:
                    send(ring_c(j, box, 4 - d, d // 2), ring_c(j, box, 2, d // 2), ("rc", j, d, 2), off(dx=d), "rc")

    def ready(n):
        for part, way in ((0, 1), (1, 7)):
            arrive(ring_a(n, zs[4], part), ("ra", n, way, 4))
        for d in (1, 3):
            arrive(size(y_=QUADS[n // 2], z_=4), ("rb", n, d, 2))
        if n % 2 == 1:
            for d in (1, 3):
                arrive(size(r=2, y_=QUADS[n // 2], z_=4), ("rc", n // 2, d, 2))

    def amp_arrived(slot, x_):
        return xbuf.at[slot, pl.ds(x_ * ROWS, ROWS), :]

    def forward_amp():
        for x_ in range(NX):
            here = amp_arrived(c, x_)
            arrive(here, ("amp", x_))
            send(here, here, "fwd", sibling, "fwd")

    send_plane(0)
    send_z(0)
    send_plane(1)
    send_z(1)
    for d in (1, 3, 2, 0):
        send_amp(d)
    arrive_plane(0)
    step_a(0, 1)
    step_a(1, 1)
    arrive_z(0)
    send_lines(0)
    arrive_plane(1)
    step_a(2, 1)
    step_a(3, 1)
    arrive_z(1)
    send_lines(1)
    step_a(0, 2)
    step_a(1, 2)
    step_a(2, 2)
    arrive_lines_b(0)
    step_b(0, 1)
    step_b(1, 1)
    arrive_lines_c(0)
    step_c(0, 1)
    step_a(3, 2)
    forward_amp()
    step_a(0, 3)
    step_a(1, 3)
    arrive_lines_b(1)
    step_b(2, 1)
    step_b(3, 1)
    arrive_lines_c(1)
    step_c(1, 1)
    step_a(2, 3)
    step_a(3, 3)
    step_b(0, 2)
    step_a(0, 4)
    step_b(1, 2)
    step_a(1, 4)
    step_c(0, 2)
    arrive(xbuf.at[1 - c], "fwd")

    def between(n, part):
        if (n, part) == (0, 0):
            step_b(2, 2)
            step_a(2, 4)
            step_b(3, 2)
            step_c(1, 2)
            step_a(3, 4)

    def panel(j, r):
        return jnp.concatenate([bb[t, j, r].reshape(VW, 128) for t in range(4)], axis=1)

    def panel_half(j, r, h):
        return jnp.concatenate([bb[t, j, r, pl.ds(2 * h, 2)].reshape(VW // 2, 128) for t in range(4)], axis=1)

    def first_sum(n):
        both = [panel(n >> 1, 2 * (n & 1) + r) for r in range(2)]
        done = jnp.concatenate([dot_t(xbuf[0], b).astype(BF16) for b in both], axis=0)
        tacc[...] += jnp.dot(jnp.concatenate(both, axis=1), done, preferred_element_type=F32)

    for n in range(2):
        ready(n)
        first_sum(n)
        between(n, 0)
        both = [panel(n >> 1, 2 * (n & 1) + r) for r in range(2)]
        turned = jnp.concatenate([dot_t(b, xbuf[1]).astype(BF16) for b in both], axis=1)
        tacc[...] += dot_t(turned, jnp.concatenate(both, axis=1))
        between(n, 1)

    for n in (2, 3):
        ready(n)
        for r in range(2):
            dn[2 * (n - 2) + r] = dot_t(xbuf[0], panel(1, 2 * (n - 2) + r)).astype(BF16)

    def half_rows(h):
        rows = pl.ds(pl.multiple_of(h * 256, 256), 256)
        part = [panel_half(1, r, h) for r in range(NX)]
        turned = jnp.concatenate([dot_t(b, xbuf[1]).astype(BF16) for b in part], axis=1)
        tacc[rows, :] += jnp.dot(
            jnp.concatenate(part, axis=1), dn[...].reshape(NX * VW, VW), preferred_element_type=F32
        ) + dot_t(turned, jnp.concatenate([panel(1, r) for r in range(NX)], axis=1))
        return rows

    rows = half_rows(1 - c)
    tswap = copy(tacc.at[rows, :], trecv, "tswap", sibling, "tswap")
    tswap.start()
    rows = half_rows(c)
    tswap.wait()
    full = (tacc[rows, :] + trecv[...]).astype(BF16)
    for t in range(4):
        sout[t] = full[:, 128 * t:128 * t + 128]

    low_self = jnp.logical_and(half == 0, c == 0)
    up_self = jnp.logical_and(jnp.logical_and(half == 1, c == 1), x >= 2)
    got = slots[("out", 0)] + x
    rows = pl.ds(pl.multiple_of(c * 256, 256), 256)
    for d in (1, 3, 2, 0):
        t = xs[d]
        move(jnp.logical_and(low_self, d == 0), sout.at[t], land_low.at[x, rows, :], got, dev(t, ybase, z, half), "low")
    for h in range(2):
        to = 2 * c + h
        move(jnp.logical_and(up_self, x == to), sout.at[:, pl.ds(128 * h, 128), :], land_up.at[x], got,
             dev(to, ybase + 2, z, half), "up")

    def mask_cols(i):
        return [jnp.where(lane < TILE, dom_ref[i, r, 2 * x], dom_ref[i, r, 2 * x + 1]).astype(F32) for r in range(8)]

    all_sent(size(r=3, y_=3, z_=5), "pa")
    for j in range(2):
        all_sent(size(t=LINE[j][1], z_=7), ("z1", j))
        all_sent(size(j=2, r=3, y_=QUADS[j], z_=4), ("li", j))
    all_sent(size(t=3, r=4, y_=4, z_=7), "ra")
    all_sent(size(t=3, r=4, y_=4, z_=5), "rb")
    all_sent(size(t=3, r=4, y_=4, z_=5), "rc")
    all_sent(xbuf.at[c], "fwd")

    for i in range(PAIRS_DEV):
        arrive(land_up.at[i], ("out", i))

    @pl.when(half == 0)
    def _():
        for i in range(PAIRS_DEV):
            masks = mask_cols(i)
            for r in range(8):
                rows_ = pl.ds(r * TILE, TILE)
                out_ref[i, rows_, :] = (land_low[i, rows_, :].astype(F32) * masks[r]).astype(BF16)

    @pl.when(half == 1)
    def _():
        for i in range(PAIRS_DEV):
            masks = mask_cols(i)
            block = land_up[mir_ref[i] % PAIRS_DEV].astype(F32)
            for t in range(4):
                turned = block[t].T
                for h in range(2):
                    out_ref[i, pl.ds(128 * t + TILE * h, TILE), :] = (
                        turned[TILE * h:TILE * h + TILE] * masks[2 * t + h]).astype(BF16)

    def most_sent(short, whole, less, group):
        @pl.when(short)
        def _():
            all_sent(less, group)

        @pl.when(jnp.logical_not(short))
        def _():
            all_sent(whole, group)

    most_sent(half == c, stg, stg.at[pl.ds(0, 3)], "amp")
    most_sent(low_self, sout, sout.at[pl.ds(0, 3)], "low")
    most_sent(up_self, sout, sout.at[pl.ds(0, 2)], "up")


def body(amplitudes, panels, domain, mirror):
    slots, sends = Slots(), Slots()
    for i in range(NX):
        slots[("amp", i)]
    for i in range(NX):
        slots[("out", i)]
    vm = pl.BlockSpec(memory_space=pltpu.VMEM)
    hbm = pl.BlockSpec(memory_space=pltpu.HBM)
    return pl.pallas_call(
        functools.partial(kernel, slots, sends),
        out_shape=jax.ShapeDtypeStruct((PAIRS_DEV, VW, ROWS), BF16),
        in_specs=[hbm] * 4,
        out_specs=vm,
        scratch_shapes=[
            pltpu.VMEM((PAIRS_DEV, ROWS, VW), BF16),
            pltpu.VMEM((2, 16, VW), BF16),
            pltpu.SMEM((PAIRS_DEV, 8, 8), jnp.int32),
            pltpu.SMEM((PAIRS_DEV,), jnp.int32),
            pltpu.VMEM((PAIRS_DEV, ROWS, VW), BF16),
            pltpu.VMEM((2, VW, VW), BF16),
            pltpu.VMEM((16, VW), BF16),
            pltpu.VMEM((4, 2, NX, NY, NZ, 16, 128), BF16),
            pltpu.VMEM((VW, VW), F32),
            pltpu.VMEM((256, VW), F32),
            pltpu.VMEM((NX, VW, VW), BF16),
            pltpu.VMEM((4, 256, 128), BF16),
            pltpu.VMEM((PAIRS_DEV, VW, ROWS), BF16),
            pltpu.VMEM((PAIRS_DEV, 4, 128, 128), BF16),
            pltpu.SemaphoreType.DMA((14,)),
            pltpu.SemaphoreType.DMA((75,)),
            pltpu.SemaphoreType.DMA((4,)),
        ],
        name="ladder",
        cost_estimate=pl.CostEstimate(flops=8 * 2**30, bytes_accessed=2 * 2**20, transcendentals=0),
        compiler_params=pltpu.CompilerParams(collective_id=0, has_side_effects=True, vmem_limit_bytes=48 * 2**20),
    )(*(pltpu.with_memory_space_constraint(a, pltpu.HBM) for a in (amplitudes, panels.reshape(2, 16, VW), domain, mirror))).astype(F32)


def solution(mesh):
    in_specs = (P("pair", "virt", None), P("virt", "pair", None), P("pair", None, None), P("pair"))
    out_specs = P("pair", None, "virt")
    return jax.shard_map(body, mesh=mesh, in_specs=in_specs, out_specs=out_specs, check_vma=False)
```

```python
import functools

import jax
import jax.numpy as jnp
from jax import lax
from jax.experimental import pallas as pl
from jax.experimental.pallas import tpu as pltpu
from jax.sharding import PartitionSpec as P

MESH = pl.DeviceIdType.MESH
NX, NY, NZ = 4, 4, 8
PAIRS_DEV, VW, TILE = 4, 512, 64
ROWS = VW // NX
PART_A = ((0, 2), (0, 1))
PART_B = (((2, 1, 0, 8),), ((1, 1, 0, 8), (2, 1, 0, 4)))
PART_C = (((3, 1, 0, 8),), ((3, 1, 0, 8), (2, 1, 4, 4)))
LINE = ((2, 2), (1, 3))
QUADS = (2, 3)
F32, BF16 = jnp.float32, jnp.bfloat16


def dot_t(a, b):
    return lax.dot_general(a, b, (((1,), (1,)), ((), ())), preferred_element_type=F32)


class Slots:
    def __init__(self):
        self.names = {}

    def __getitem__(self, name):
        return self.names.setdefault(name, len(self.names))


def kernel(slots, sends, amp_hbm, pan_hbm, dom_hbm, mir_hbm, out_ref,
           amp_ref, pan_ref, dom_ref, mir_ref, stg, xbuf, pst, bb, tacc, trecv, dn, sout, land_low, land_up,
           send_sem, recv_sem, loc_sem):
    x = lax.axis_index("virt")
    p = lax.axis_index("pair")
    c = p % 2
    z = (p // 2) % NZ
    y = p // (2 * NZ)
    half = y // 2
    ybase = y % 2

    xs = [(x + d) % NX for d in range(NX)]
    ys = [(y + d) % NY for d in range(NY)]
    zs = [(z + d) % NZ for d in range(NZ)]

    def dev(x_, y_, z_, c_):
        return ((y_ * NZ + z_) * 2 + c_, x_)

    def off(dx=0, dy=0, dz=0):
        return dev(xs[dx], ys[dy], zs[dz], c)

    sibling = dev(x, y, z, 1 - c)

    def copy(src, dst, name, device, group):
        return pltpu.make_async_remote_copy(
            src_ref=src, dst_ref=dst, send_sem=send_sem.at[sends[group]], recv_sem=recv_sem.at[slots[name]],
            device_id=device, device_id_type=MESH)

    def send(src, dst, name, device, group):
        copy(src, dst, name, device, group).start()

    def arrive(ref, name):
        pltpu.make_async_copy(ref, ref, recv_sem.at[slots[name]]).wait()

    def all_sent(ref, group):
        pltpu.make_async_copy(ref, ref, send_sem.at[sends[group]]).wait()

    def size(t=1, j=1, r=1, y_=1, z_=1):
        return bb.at[pl.ds(0, t), pl.ds(0, j), pl.ds(0, r), pl.ds(0, y_), pl.ds(0, z_)]

    loads = [pltpu.make_async_copy(src, dst, loc_sem.at[i]) for i, (src, dst) in enumerate(
        ((dom_hbm, dom_ref), (mir_hbm, mir_ref), (pan_hbm, pan_ref), (amp_hbm, amp_ref)))]
    for load in loads:
        load.start()

    barrier = pltpu.get_barrier_semaphore()
    peers = [off(dz=d) for d in range(1, NZ)]
    peers += [off(dx=dx, dy=dy) for dx in range(NX) for dy in (1, 3)]
    peers += [dev(xs[dx], ys[dy], z, (c, 1 - c)[dc])
              for dx in range(NX) for dy in (0, 2) for dc in range(2) if (dx, dy, dc) != (0, 0, 0)]
    for peer in peers:
        pl.semaphore_signal(barrier, inc=1, device_id=peer, device_id_type=MESH)

    tacc[...] = jnp.zeros_like(tacc)
    for load in loads:
        load.wait()

    lane = lax.broadcasted_iota(jnp.int32, (1, 128), 1)
    order = []
    for i in range(PAIRS_DEV):
        found = jnp.int32(0)
        for q in range(PAIRS_DEV):
            found = jnp.where(mir_ref[q] % PAIRS_DEV == i, jnp.int32(q), found)
        order.append(jnp.where(half == 0, jnp.int32(i), found))
    for i in range(PAIRS_DEV):
        for h in range(2):
            row = 2 * x + h
            parts = [jnp.where(lane < TILE, dom_ref[order[i], row, 2 * t], dom_ref[order[i], row, 2 * t + 1])
                     for t in range(4)]
            mask = jnp.concatenate(parts, axis=1).astype(F32)
            rows = pl.ds(h * TILE, TILE)
            stg[i, rows, :] = (amp_ref[order[i], rows, :].astype(F32) * mask).astype(BF16)

    def amp_slot(x_):
        return xbuf.at[half, pl.ds(pl.multiple_of(x_ * ROWS, ROWS), ROWS), :]

    def move(here, src, dst, name, device, group):
        @pl.when(jnp.logical_not(here))
        def _():
            pltpu.make_async_remote_copy(
                src_ref=src, dst_ref=dst, send_sem=send_sem.at[sends[group]], recv_sem=recv_sem.at[name],
                device_id=device, device_id_type=MESH).start()

        @pl.when(here)
        def _():
            pltpu.make_async_copy(src, dst, recv_sem.at[name]).start()

    def send_amp(d):
        i = xs[d]
        move(jnp.logical_and(half == c, d == 0), stg.at[i], amp_slot(x), slots[("amp", 0)] + x,
             dev(i, ybase + 2 * c, z, half), "amp")

    pl.semaphore_wait(barrier, len(peers))

    swap = copy(pan_ref.at[1 - c], pst, "swap", sibling, "swap")
    swap.start()
    swap.wait()
    mine = pan_ref[c].astype(F32)
    other = pst[...].astype(F32)
    first = jnp.where(c == 0, mine, other)
    second = jnp.where(c == 0, other, mine)
    for j in range(2):
        rows16 = jnp.concatenate([first[8 * j:8 * j + 8], second[8 * j:8 * j + 8]], axis=0).astype(BF16)
        for t in range(4):
            bb[t, j, 0, y, z] = rows16[:, 128 * t:128 * t + 128]

    def plane_a(j, r, y_):
        return bb.at[pl.ds(*PART_A[j]), j, r, y_, z]

    def send_plane(j):
        for dy in (0, 1, 3, 2):
            for dx in (0, 1, 3, 2):
                if (dx, dy) != (0, 0):
                    send(plane_a(j, 0, y), plane_a(j, -dx % NX, y), ("pa", j), off(dx=dx, dy=dy), "pa")

    def arrive_plane(j):
        arrive(size(t=PART_A[j][1], y_=3, z_=5), ("pa", j))

    def line_z(j, z_):
        return bb.at[pl.ds(*LINE[j]), j, 0, y, z_]

    def send_z(j):
        for d in (4, 3, 5, 2, 6, 1, 7):
            send(line_z(j, z), line_z(j, z), ("z1", j), off(dz=d), ("z1", j))

    def arrive_z(j):
        arrive(size(t=LINE[j][1], z_=7), ("z1", j))

    def line(box, j, r, y_):
        return bb.at[pl.ds(box[0], box[1]), j, r, y_, pl.ds(box[2], box[3])]

    def send_lines(j):
        for d in (2, 1, 3):
            for box in PART_B[j]:
                send(line(box, j, 0, y), line(box, j, -d % NX, y), ("lb", j), off(dx=d), ("li", j))
            for box in PART_C[j]:
                send(line(box, j, 0, y), line(box, j, 0, y), ("lc", j), off(dy=d), ("li", j))

    def arrive_lines_b(j):
        arrive(size(y_=3, r=QUADS[j], z_=4), ("lb", j))

    def arrive_lines_c(j):
        arrive(size(y_=3, r=QUADS[j], z_=4), ("lc", j))

    def ring_a(n, z_, part=None):
        r = pl.ds(2 * (n % 2), 2) if part is None else pl.ds(2 * (n % 2) + part, 1)
        return bb.at[pl.ds(*PART_A[n // 2]), n // 2, r, :, z_]

    def step_a(n, s):
        for way, sign, part in ((1, -1, 0), (7, 1, 1)):
            here = zs[sign * (s - 1)]
            if s > 1:
                arrive(ring_a(n, here), ("ra", n, way, s - 1))
            ref = ring_a(n, here, part if s == 4 else None)
            send(ref, ref, ("ra", n, way, s), off(dz=way), "ra")

    def ring_b(n, box, y_, part=None):
        r = pl.ds(2 * (n % 2), 2) if part is None else pl.ds(2 * (n % 2) + part, 1)
        return bb.at[pl.ds(box[0], box[1]), n // 2, r, y_, pl.ds(box[2], box[3])]

    def step_b(n, s):
        for d in (1, 3):
            if s > 1:
                arrive(size(r=2, y_=QUADS[n // 2], z_=4), ("rb", n, d, 1))
            for box in PART_B[n // 2]:
                ref = ring_b(n, box, y) if s == 1 else ring_b(n, box, ys[-d], d // 2)
                send(ref, ref, ("rb", n, d, s), off(dy=d), "rb")

    def ring_c(j, box, r, part=None):
        some = slice(None) if part is None else pl.ds(2 * part, 2)
        return bb.at[pl.ds(box[0], box[1]), j, r, some, pl.ds(box[2], box[3])]

    def step_c(j, s):
        for d in (1, 3):
            if s > 1:
                arrive(size(r=4, y_=QUADS[j], z_=4), ("rc", j, d, 1))
            for box in PART_C[j]:
                if s == 1:
                    send(ring_c(j, box, 0), ring_c(j, box, 4 - d), ("rc", j, d, 1), off(dx=d), "rc")
                else:
                    send(ring_c(j, box, 4 - d, d // 2), ring_c(j, box, 2, d // 2), ("rc", j, d, 2), off(dx=d), "rc")

    def ready(n):
        for part, way in ((0, 1), (1, 7)):
            arrive(ring_a(n, zs[4], part), ("ra", n, way, 4))
        for d in (1, 3):
            arrive(size(y_=QUADS[n // 2], z_=4), ("rb", n, d, 2))
        if n % 2 == 1:
            for d in (1, 3):
                arrive(size(r=2, y_=QUADS[n // 2], z_=4), ("rc", n // 2, d, 2))

    def amp_arrived(slot, x_):
        return xbuf.at[slot, pl.ds(x_ * ROWS, ROWS), :]

    def forward_amp():
        for x_ in range(NX):
            here = amp_arrived(c, x_)
            arrive(here, ("amp", x_))
            send(here, here, "fwd", sibling, "fwd")

    send_plane(0)
    send_z(0)
    send_plane(1)
    send_z(1)
    for d in (2, 1, 3, 0):
        send_amp(d)
    arrive_plane(0)
    step_a(0, 1)
    step_a(1, 1)
    arrive_z(0)
    send_lines(0)
    arrive_plane(1)
    step_a(2, 1)
    step_a(3, 1)
    arrive_z(1)
    send_lines(1)
    step_a(0, 2)
    step_a(1, 2)
    step_a(2, 2)
    arrive_lines_b(0)
    step_b(0, 1)
    step_b(1, 1)
    arrive_lines_c(0)
    step_c(0, 1)
    step_a(3, 2)
    forward_amp()
    step_a(0, 3)
    step_a(1, 3)
    arrive_lines_b(1)
    step_b(2, 1)
    step_b(3, 1)
    arrive_lines_c(1)
    step_c(1, 1)
    step_a(2, 3)
    step_a(3, 3)
    step_b(0, 2)
    step_a(0, 4)
    step_b(1, 2)
    step_a(1, 4)
    step_c(0, 2)
    arrive(xbuf.at[1 - c], "fwd")

    def between(n, part):
        if (n, part) == (0, 0):
            step_b(2, 2)
            step_a(2, 4)
            step_b(3, 2)
            step_c(1, 2)
            step_a(3, 4)

    def panel(j, r):
        return jnp.concatenate([bb[t, j, r].reshape(VW, 128) for t in range(4)], axis=1)

    def panel_half(j, r, h):
        return jnp.concatenate([bb[t, j, r, pl.ds(2 * h, 2)].reshape(VW // 2, 128) for t in range(4)], axis=1)

    def first_sum(n):
        both = [panel(n >> 1, 2 * (n & 1) + r) for r in range(2)]
        done = jnp.concatenate([dot_t(xbuf[0], b).astype(BF16) for b in both], axis=0)
        tacc[...] += jnp.dot(jnp.concatenate(both, axis=1), done, preferred_element_type=F32)

    for n in range(2):
        ready(n)
        first_sum(n)
        between(n, 0)
        both = [panel(n >> 1, 2 * (n & 1) + r) for r in range(2)]
        turned = jnp.concatenate([dot_t(b, xbuf[1]).astype(BF16) for b in both], axis=1)
        tacc[...] += dot_t(turned, jnp.concatenate(both, axis=1))
        between(n, 1)

    for n in (2, 3):
        ready(n)
        for r in range(2):
            dn[2 * (n - 2) + r] = dot_t(xbuf[0], panel(1, 2 * (n - 2) + r)).astype(BF16)

    def half_rows(h):
        rows = pl.ds(pl.multiple_of(h * 256, 256), 256)
        part = [panel_half(1, r, h) for r in range(NX)]
        turned = jnp.concatenate([dot_t(b, xbuf[1]).astype(BF16) for b in part], axis=1)
        tacc[rows, :] += jnp.dot(
            jnp.concatenate(part, axis=1), dn[...].reshape(NX * VW, VW), preferred_element_type=F32
        ) + dot_t(turned, jnp.concatenate([panel(1, r) for r in range(NX)], axis=1))
        return rows

    rows = half_rows(1 - c)
    tswap = copy(tacc.at[rows, :], trecv, "tswap", sibling, "tswap")
    tswap.start()
    rows = half_rows(c)
    tswap.wait()
    full = (tacc[rows, :] + trecv[...]).astype(BF16)
    for t in range(4):
        sout[t] = full[:, 128 * t:128 * t + 128]

    low_self = jnp.logical_and(half == 0, c == 0)
    up_self = jnp.logical_and(jnp.logical_and(half == 1, c == 1), x >= 2)
    got = slots[("out", 0)] + x
    rows = pl.ds(pl.multiple_of(c * 256, 256), 256)
    for d in (2, 1, 3, 0):
        t = xs[d]
        move(jnp.logical_and(low_self, d == 0), sout.at[t], land_low.at[x, rows, :], got, dev(t, ybase, z, half), "low")
    for h in range(2):
        to = 2 * c + h
        move(jnp.logical_and(up_self, x == to), sout.at[:, pl.ds(128 * h, 128), :], land_up.at[x], got,
             dev(to, ybase + 2, z, half), "up")

    def mask_cols(i):
        return [jnp.where(lane < TILE, dom_ref[i, r, 2 * x], dom_ref[i, r, 2 * x + 1]).astype(F32) for r in range(8)]

    all_sent(size(r=3, y_=3, z_=5), "pa")
    for j in range(2):
        all_sent(size(t=LINE[j][1], z_=7), ("z1", j))
        all_sent(size(j=2, r=3, y_=QUADS[j], z_=4), ("li", j))
    all_sent(size(t=3, r=4, y_=4, z_=7), "ra")
    all_sent(size(t=3, r=4, y_=4, z_=5), "rb")
    all_sent(size(t=3, r=4, y_=4, z_=5), "rc")
    all_sent(xbuf.at[c], "fwd")

    for i in range(PAIRS_DEV):
        arrive(land_up.at[i], ("out", i))

    @pl.when(half == 0)
    def _():
        for i in range(PAIRS_DEV):
            masks = mask_cols(i)
            for r in range(8):
                rows_ = pl.ds(r * TILE, TILE)
                out_ref[i, rows_, :] = (land_low[i, rows_, :].astype(F32) * masks[r]).astype(BF16)

    @pl.when(half == 1)
    def _():
        for i in range(PAIRS_DEV):
            masks = mask_cols(i)
            block = land_up[mir_ref[i] % PAIRS_DEV].astype(F32)
            for t in range(4):
                turned = block[t].T
                for h in range(2):
                    out_ref[i, pl.ds(128 * t + TILE * h, TILE), :] = (
                        turned[TILE * h:TILE * h + TILE] * masks[2 * t + h]).astype(BF16)

    def most_sent(short, whole, less, group):
        @pl.when(short)
        def _():
            all_sent(less, group)

        @pl.when(jnp.logical_not(short))
        def _():
            all_sent(whole, group)

    most_sent(half == c, stg, stg.at[pl.ds(0, 3)], "amp")
    most_sent(low_self, sout, sout.at[pl.ds(0, 3)], "low")
    most_sent(up_self, sout, sout.at[pl.ds(0, 2)], "up")


def body(amplitudes, panels, domain, mirror):
    slots, sends = Slots(), Slots()
    for i in range(NX):
        slots[("amp", i)]
    for i in range(NX):
        slots[("out", i)]
    vm = pl.BlockSpec(memory_space=pltpu.VMEM)
    hbm = pl.BlockSpec(memory_space=pltpu.HBM)
    return pl.pallas_call(
        functools.partial(kernel, slots, sends),
        out_shape=jax.ShapeDtypeStruct((PAIRS_DEV, VW, ROWS), BF16),
        in_specs=[hbm] * 4,
        out_specs=vm,
        scratch_shapes=[
            pltpu.VMEM((PAIRS_DEV, ROWS, VW), BF16),
            pltpu.VMEM((2, 16, VW), BF16),
            pltpu.SMEM((PAIRS_DEV, 8, 8), jnp.int32),
            pltpu.SMEM((PAIRS_DEV,), jnp.int32),
            pltpu.VMEM((PAIRS_DEV, ROWS, VW), BF16),
            pltpu.VMEM((2, VW, VW), BF16),
            pltpu.VMEM((16, VW), BF16),
            pltpu.VMEM((4, 2, NX, NY, NZ, 16, 128), BF16),
            pltpu.VMEM((VW, VW), F32),
            pltpu.VMEM((256, VW), F32),
            pltpu.VMEM((NX, VW, VW), BF16),
            pltpu.VMEM((4, 256, 128), BF16),
            pltpu.VMEM((PAIRS_DEV, VW, ROWS), BF16),
            pltpu.VMEM((PAIRS_DEV, 4, 128, 128), BF16),
            pltpu.SemaphoreType.DMA((14,)),
            pltpu.SemaphoreType.DMA((75,)),
            pltpu.SemaphoreType.DMA((4,)),
        ],
        name="ladder",
        cost_estimate=pl.CostEstimate(flops=8 * 2**30, bytes_accessed=2 * 2**20, transcendentals=0),
        compiler_params=pltpu.CompilerParams(collective_id=0, has_side_effects=True, vmem_limit_bytes=48 * 2**20),
    )(*(pltpu.with_memory_space_constraint(a, pltpu.HBM) for a in (amplitudes, panels.reshape(2, 16, VW), domain, mirror))).astype(F32)


def solution(mesh):
    in_specs = (P("pair", "virt", None), P("virt", "pair", None), P("pair", None, None), P("pair"))
    out_specs = P("pair", None, "virt")
    return jax.shard_map(body, mesh=mesh, in_specs=in_specs, out_specs=out_specs, check_vma=False)
```
